32 devices in a mesh: seq: 8 (over z, x), tp: 4 (over y, core).
Axes of the slice: x: 2, y: 2, z: 4, core: 2. Of those that a mesh axis runs over, the one named last changes fastest.
Arguments:
- tokens: bfloat16 [4096, 2048], P('seq', 'tp'), may hold values from -6 to 6
- w_first: bfloat16 [8, 512, 512], P('seq'), may hold values from -0.25 to 0.25
- second_factor_weight: bfloat16 [512, 8, 8], P('seq'), may hold values from -2 to 2
- w_up: bfloat16 [64, 2, 128, 128], P('tp'), may hold values from -0.375 to 0.375
- w_self: bfloat16 [6, 64, 128, 128], P(None, 'tp'), may hold values from -0.375 to 0.375
- w_cross: bfloat16 [6, 64, 128, 128], P(None, 'tp'), may hold values from -0.375 to 0.375
- w_down: bfloat16 [64, 2, 128, 128], P('tp'), may hold values from -0.1875 to 0.1875
- block_pairs: int32 [64, 2], P('tp'), may hold values from 0 to 15, all different within a row
- cotangent: bfloat16 [4096, 2048], P('seq', 'tp'), may hold values from -6 to 6
Outputs:
- layer_out: bfloat16 [4096, 2048], P('seq', 'tp')
- grad_tokens: bfloat16 [4096, 2048], P('seq', 'tp')
- grad_first: float32 [8, 512, 512], P('seq')
- gradient_second_factor: float32 [512, 8, 8], P('seq')
- grad_self: float32 [6, 64, 128, 128], P(None, 'tp', 'seq')
- grad_cross: float32 [6, 64, 128, 128], P(None, 'tp', 'seq')
The draws below stay inside these ranges and needn't reach their ends.
Inputs may be any that keep to these rules, and one draw needn't show every extreme that they name: `block_pairs`: each row names two different input blocks, and every one of the 16 input blocks is named by some row.
All inputs are finite; a program needn't handle non-finite values.
Results may differ from the reference program's by a relative error of at most 0.019.
Values may be sent and summed in bfloat16 or wider, within the bound.
A program may use at most 128 MiB of HBM per device.

```python
import math
import jax
import jax.numpy as jnp
from jax import lax

MODEL_DIMENSION = 2048
BLK = 128
B = 512
LEVELS = 6
SEQ_DEV = 512
SEQUENCE_TOKENS = 4096
NB = 8
HB = 64
IB = 16
N_SEQ = 8


def levels(rng, shape, cuts, smallest, top_value):
    def one(dim, parts):
        steps = jax.random.uniform(jax.random.fold_in(jax.random.fold_in(rng, 6), dim), (parts,), jnp.float32, smallest / len(cuts), top_value / len(cuts))
        return jnp.repeat(jnp.exp(steps), shape[dim] // parts).reshape((-1,) + (1,) * (len(shape) - dim - 1))

    loudness = one(*cuts[0])
    for cut in cuts[1:]:
        loudness = loudness * one(*cut)
    return loudness


def picks_of(rng, rows, number_of, top, lift):
    order = jax.random.permutation(jax.random.fold_in(rng, 1), number_of)
    favour = order
    for power in range(3):
        favour = favour * favour // number_of
    favour = favour * lift // number_of
    tickets = jax.random.randint(jax.random.fold_in(rng, 2), (rows, number_of), 0, 4096) + favour
    holders = jax.random.permutation(jax.random.fold_in(rng, 3), rows)[jnp.arange(number_of) % rows]
    tickets = jnp.where(jnp.arange(rows)[:, None] == holders[None, :], 1 << 14, tickets)
    merit = tickets * number_of + jnp.arange(number_of)
    return lax.top_k(merit.astype(jnp.int32), top)[1].astype(jnp.int32)


def noise(key, extent, scale, limit, split=(), kind=jnp.bfloat16):
    entries = jax.random.normal(key, extent, jnp.float32) * scale
    if len(split) > 0:
        entries = levels(key, extent, split, -0.22, 0.18) * entries
    return jnp.clip(entries, min=-limit, max=limit).astype(kind)


def setup_inputs(seed: int = 0) -> dict:
    arg_keys = jax.random.split(jax.random.key(seed), 10)
    return {
        "tokens": noise(arg_keys[0], (SEQUENCE_TOKENS, MODEL_DIMENSION), 1.0, 6.0, ((0, 8), (1, 4))),
        "w_first": noise(arg_keys[1], (NB, B, B), B ** -0.5, 0.25, ((0, 8),)),
        "second_factor_weight": noise(arg_keys[2], (B, NB, NB), NB ** -0.5, 2.0, ((0, 8),)),
        "w_up": noise(arg_keys[3], (HB, 2, BLK, BLK), (2 * BLK) ** -0.5, 0.375, ((0, 4),)),
        "w_self": noise(arg_keys[4], (LEVELS, HB, BLK, BLK), (2 * BLK) ** -0.5, 0.375, ((1, 4),)),
        "w_cross": noise(arg_keys[5], (LEVELS, HB, BLK, BLK), (2 * BLK) ** -0.5, 0.375, ((1, 4),)),
        "w_down": noise(arg_keys[6], (HB, 2, BLK, BLK), (2 * HB * BLK // IB) ** -0.5, 0.1875, ((0, 4),)),
        "block_pairs": picks_of(arg_keys[7], HB, IB, 2, 0),
        "cotangent": noise(arg_keys[8], (SEQUENCE_TOKENS, MODEL_DIMENSION), 1.0, 6.0, ((0, 8), (1, 4))),
    }


def gelu_tanh(value):
    return jax.nn.gelu(value, approximate=True)

def swap_partner(state, level):
    span = 2 ** level
    shape = state.shape
    folded = state.reshape(shape[0], shape[1] // (2 * span), 2, span, shape[2])
    return jnp.flip(folded, axis=2).reshape(shape)

def reference(tokens, w_first, second_factor_weight, w_up, w_self, w_cross, w_down, block_pairs, cotangent):
    grouped = tokens.reshape(NB, B, MODEL_DIMENSION).astype(jnp.float32)
    first_factor_output = jnp.einsum('acb,abd->acd', w_first.astype(jnp.float32), grouped).astype(jnp.bfloat16)
    mixed_tokens = jnp.einsum('vyi,ivz->yvz', second_factor_weight.astype(jnp.float32), first_factor_output.astype(jnp.float32)).astype(jnp.bfloat16).reshape(SEQUENCE_TOKENS, MODEL_DIMENSION)
    hidden_in = (tokens.astype(jnp.float32) + mixed_tokens.astype(jnp.float32)).astype(jnp.bfloat16)
    flat_pairs = block_pairs.reshape(-1)
    chosen = (block_pairs[:, :, None] == jnp.arange(IB, dtype=jnp.int32)[None, None, :]).astype(jnp.float32)
    up_full = w_up.astype(jnp.float32)
    down_full = w_down.astype(jnp.float32)
    self_full = w_self.astype(jnp.float32)
    cross_full = w_cross.astype(jnp.float32)

    def mlp_block(carry, rows_in):
        grads_self, grads_cross = carry
        hid_rows, cot_rows = rows_in
        count = hid_rows.shape[0]
        picked = jnp.take(hid_rows.reshape(count, IB, BLK), flat_pairs, axis=1).reshape(count, HB, 2, BLK)
        state = jnp.einsum('rjkc,jkce->rje', picked.astype(jnp.float32), up_full).astype(jnp.bfloat16)
        states = [state]
        for level_at in range(LEVELS):
            partner = swap_partner(state, level_at)
            state = (jnp.einsum('rjc,jce->rje', state.astype(jnp.float32), self_full[level_at]) + jnp.einsum('rjc,jce->rje', partner.astype(jnp.float32), cross_full[level_at])).astype(jnp.bfloat16)
            states.append(state)
        top = state.astype(jnp.float32)
        activated = gelu_tanh(top).astype(jnp.bfloat16)
        pieces = jnp.einsum('rjc,jkce->rjke', activated.astype(jnp.float32), down_full)
        down_out = jnp.einsum('rjke,jki->rie', pieces, chosen).reshape(count, MODEL_DIMENSION)
        layer_rows = (hid_rows.astype(jnp.float32) + down_out).astype(jnp.bfloat16)
        grad_picked = jnp.take(cot_rows.reshape(count, IB, BLK), flat_pairs, axis=1).reshape(count, HB, 2, BLK)
        grad_act = jnp.einsum('rjke,jkce->rjc', grad_picked.astype(jnp.float32), down_full)
        _, pull = jax.vjp(gelu_tanh, top)
        grad_state = pull(grad_act)[0].astype(jnp.bfloat16)
        self_terms = [None] * LEVELS
        cross_terms = [None] * LEVELS
        for level_at in reversed(range(LEVELS)):
            below = states[level_at].astype(jnp.float32)
            upper = grad_state.astype(jnp.float32)
            self_terms[level_at] = jnp.einsum('rjc,rje->jce', below, upper)
            cross_terms[level_at] = jnp.einsum('rjc,rje->jce', swap_partner(below, level_at), upper)
            across = jnp.einsum('rje,jce->rjc', upper, cross_full[level_at])
            grad_state = (jnp.einsum('rje,jce->rjc', upper, self_full[level_at]) + swap_partner(across, level_at)).astype(jnp.bfloat16)
        back_pieces = jnp.einsum('rje,jkce->rjkc', grad_state.astype(jnp.float32), up_full)
        spread = jnp.einsum('rjkc,jki->ric', back_pieces, chosen).reshape(count, MODEL_DIMENSION)
        grad_rows = (cot_rows.astype(jnp.float32) + spread).astype(jnp.bfloat16)
        carry_out = (grads_self + jnp.stack(self_terms), grads_cross + jnp.stack(cross_terms))
        return (carry_out, (layer_rows, grad_rows))
    zeros_start = jnp.zeros((LEVELS, HB, BLK, BLK), jnp.float32)
    sums, outputs = lax.scan(mlp_block, (zeros_start, zeros_start), (hidden_in.reshape(N_SEQ, SEQ_DEV, MODEL_DIMENSION), cotangent.reshape(N_SEQ, SEQ_DEV, MODEL_DIMENSION)))
    layer_out = outputs[0].reshape(SEQUENCE_TOKENS, MODEL_DIMENSION)
    grad_hidden = outputs[1].reshape(SEQUENCE_TOKENS, MODEL_DIMENSION)
    token_scale = 1.0 / math.sqrt(SEQUENCE_TOKENS)
    model_width_scale = 1.0 / math.sqrt(MODEL_DIMENSION)
    gradient_group_rows = grad_hidden.reshape(NB, B, MODEL_DIMENSION).astype(jnp.float32)
    gradient_first_output = jnp.einsum('emj,meg->jeg', second_factor_weight.astype(jnp.float32), gradient_group_rows).astype(jnp.bfloat16)
    gradient_second_factor = jnp.einsum('tfm,lfm->ftl', gradient_group_rows, first_factor_output.astype(jnp.float32)) * model_width_scale
    grad_first = jnp.einsum('acd,abd->acb', gradient_first_output.astype(jnp.float32), grouped) * model_width_scale
    grad_mix = jnp.einsum('acb,acd->abd', w_first.astype(jnp.float32), gradient_first_output.astype(jnp.float32)).reshape(SEQUENCE_TOKENS, MODEL_DIMENSION)
    grad_tokens = (grad_hidden.astype(jnp.float32) + grad_mix).astype(jnp.bfloat16)
    return (layer_out, grad_tokens, grad_first, gradient_second_factor, sums[0] * token_scale, sums[1] * token_scale)
```

```python
import functools
import math

import jax
import jax.numpy as jnp
from jax import lax
from jax.experimental import pallas as pl
from jax.experimental.pallas import tpu as pltpu
from jax.sharding import PartitionSpec as P

BF = jnp.bfloat16
F32 = jnp.float32
VMEM_BYTES = 56 * 1024 * 1024


def dot(left, right, contract):
    return lax.dot_general(left, right, (contract, ((), ())), preferred_element_type=F32)


def dot_nn(left, right):
    return dot(left, right, ((1,), (0,)))


def dot_nt(left, right):
    return dot(left, right, ((1,), (1,)))


def dot_tn(left, right):
    return dot(left, right, ((0,), (0,)))


def partner_2(value, axis, bit):
    mask = 2**bit
    pairs = [(source, source ^ mask) for source in range(lax.axis_size(axis))]
    return lax.ppermute(value, axis, pairs)


def lanes(index, width):
    return pl.ds(pl.multiple_of(index * width, width), width)


def pair_of(index, level):
    low = 2**level
    first = (index // low) * (2 * low) + index % low
    return first, first + low


def pair_matrix(w_self, w_cross, first, second):
    top = jnp.concatenate([w_self[0, first], w_cross[0, second]], axis=1)
    bottom = jnp.concatenate([w_cross[0, first], w_self[0, second]], axis=1)
    return jnp.concatenate([top, bottom], axis=0)


def side_by_side(ref, first, second, width):
    return jnp.concatenate([ref[:, lanes(first, width)], ref[:, lanes(second, width)]], axis=1)


def up_kernel(levels, slots, width, pairs, hidden, w_up, *refs):
    w_self, w_cross, states = refs[:levels], refs[levels : 2 * levels], refs[2 * levels :]

    @pl.loop(0, slots)
    def _(j):
        both = side_by_side(hidden, pairs[j, 0], pairs[j, 1], width)
        matrix = jnp.concatenate([w_up[j, 0], w_up[j, 1]], axis=0)
        states[0][:, lanes(j, width)] = dot_nn(both, matrix).astype(BF)

    for level in range(levels):

        @pl.loop(0, slots // 2)
        def _(index):
            first, second = pair_of(index, level)
            both = side_by_side(states[level], first, second, width)
            result = dot_nn(both, pair_matrix(w_self[level], w_cross[level], first, second)).astype(BF)
            states[level + 1][:, lanes(first, width)] = result[:, :width]
            states[level + 1][:, lanes(second, width)] = result[:, width:]


def across_kernel(slots, width, state, partner, w_self, w_cross, out):
    @pl.loop(0, slots)
    def _(j):
        both = jnp.concatenate([state[:, lanes(j, width)], partner[:, lanes(j, width)]], axis=1)
        matrix = jnp.concatenate([w_self[0, j], w_cross[0, j]], axis=0)
        out[:, lanes(j, width)] = dot_nn(both, matrix).astype(BF)


def top_kernel(
    slots, width, pairs, state, partner, w_self, w_cross, w_down, cotangent, down, grad, send, total
):
    total[...] = jnp.zeros_like(total)

    @pl.loop(0, slots)
    def _(j):
        first, second = pairs[j, 0], pairs[j, 1]
        both = jnp.concatenate([state[:, lanes(j, width)], partner[:, lanes(j, width)]], axis=1)
        matrix = jnp.concatenate([w_self[0, j], w_cross[0, j]], axis=0)
        top = dot_nn(both, matrix).astype(BF).astype(F32)
        root = math.sqrt(2.0 / math.pi)
        square = top * top
        bend = jnp.tanh(root * (top + 0.044715 * (square * top)))
        active = (0.5 * top * (1.0 + bend)).astype(BF)
        slope = 0.5 * (1.0 + bend) + 0.5 * top * (1.0 - bend * bend) * (
            root * (1.0 + (3 * 0.044715) * square)
        )
        w_both = jnp.concatenate([w_down[j, 0], w_down[j, 1]], axis=1)
        pieces = dot_nn(active, w_both)
        total[:, lanes(first, width)] += pieces[:, :width]
        total[:, lanes(second, width)] += pieces[:, width:]
        grad_act = dot_nt(side_by_side(cotangent, first, second, width), w_both)
        grad_top = (grad_act * slope).astype(BF)
        grad[:, lanes(j, width)] = grad_top
        send[:, lanes(j, width)] = dot_nt(grad_top, w_cross[0, j]).astype(BF)

    down[...] = total[...].astype(BF)


def across_grad_kernel(slots, width, state, partner, grad, terms):
    @pl.loop(0, slots)
    def _(j):
        both = jnp.concatenate([state[:, lanes(j, width)], partner[:, lanes(j, width)]], axis=1)
        result = dot_tn(both, grad[:, lanes(j, width)]).astype(BF)
        terms[0, j] = result[:width]
        terms[1, j] = result[width:]


def middle_kernel(slots, width, grad, incoming, w_self, w_cross_below, out, send):
    @pl.loop(0, slots)
    def _(j):
        own = dot_nt(grad[:, lanes(j, width)], w_self[0, j])
        result = (own + incoming[:, lanes(j, width)].astype(F32)).astype(BF)
        out[:, lanes(j, width)] = result
        send[:, lanes(j, width)] = dot_nt(result, w_cross_below[0, j]).astype(BF)


def down_kernel(levels, slots, width, pairs, grad, incoming, w_self_above, w_up, *refs):
    w_self, w_cross = refs[:levels], refs[levels : 2 * levels]
    grads = refs[2 * levels : 3 * levels + 1]
    spread, total = refs[3 * levels + 1 :]

    @pl.loop(0, slots)
    def _(j):
        own = dot_nt(grad[:, lanes(j, width)], w_self_above[0, j])
        result = own + incoming[:, lanes(j, width)].astype(F32)
        grads[levels][:, lanes(j, width)] = result.astype(BF)

    for level in reversed(range(levels)):

        @pl.loop(0, slots // 2)
        def _(index):
            first, second = pair_of(index, level)
            both = side_by_side(grads[level + 1], first, second, width)
            result = dot_nt(both, pair_matrix(w_self[level], w_cross[level], first, second)).astype(BF)
            grads[level][:, lanes(first, width)] = result[:, :width]
            grads[level][:, lanes(second, width)] = result[:, width:]

    total[...] = jnp.zeros_like(total)

    @pl.loop(0, slots)
    def _(j):
        matrix = jnp.concatenate([w_up[j, 0], w_up[j, 1]], axis=0)
        pieces = dot_nt(grads[0][:, lanes(j, width)], matrix)
        total[:, lanes(pairs[j, 0], width)] += pieces[:, :width]
        total[:, lanes(pairs[j, 1], width)] += pieces[:, width:]

    spread[...] = total[...].astype(BF)


def pair_grad_kernel(level, slots, width, state, grad, terms):
    @pl.loop(0, slots // 2)
    def _(index):
        first, second = pair_of(index, level)
        result = dot_tn(
            side_by_side(state, first, second, width), side_by_side(grad, first, second, width)
        ).astype(BF)
        terms[0, first] = result[:width, :width]
        terms[1, second] = result[:width, width:]
        terms[1, first] = result[width:, :width]
        terms[0, second] = result[width:, width:]


def whole(array):
    return pl.BlockSpec(array.shape, lambda i: (0,) * array.ndim)


def level_of(array, level):
    return pl.BlockSpec((1,) + array.shape[1:], lambda i: (level, 0, 0, 0))


def rows_of(shape, tile):
    return pl.BlockSpec((tile, shape[1]), lambda i: (i, 0))


def call(kernel, steps, operands, in_specs, out_shapes, out_specs, flops, scratch=()):
    moved = sum(x.size * x.dtype.itemsize for x in operands[:4])
    moved += sum(math.prod(x.shape) * x.dtype.itemsize for x in out_shapes)
    return pl.pallas_call(
        kernel,
        grid=(steps,),
        in_specs=in_specs,
        out_specs=out_specs,
        out_shape=out_shapes,
        scratch_shapes=scratch,
        compiler_params=pltpu.CompilerParams(vmem_limit_bytes=VMEM_BYTES),
        cost_estimate=pl.CostEstimate(flops=flops, bytes_accessed=moved, transcendentals=0),
    )(*operands)


def per_device(
    tokens, w_first, second_factor_weight, w_up, w_self, w_cross, w_down, block_pairs, cotangent
):
    seq_len, width_local = tokens.shape
    levels, slots, width, _ = w_self.shape
    model_width = width_local * lax.axis_size("tp")
    local = slots.bit_length() - 1
    hidden_width = slots * width
    total_tokens = seq_len * lax.axis_size("seq")
    token_scale = 1.0 / math.sqrt(total_tokens)
    model_width_scale = 1.0 / math.sqrt(model_width)
    positions, groups, _ = second_factor_weight.shape
    tile = seq_len // 2
    steps = 2
    smem = pl.BlockSpec(memory_space=pltpu.SMEM)
    state_shape = jax.ShapeDtypeStruct((seq_len, hidden_width), BF)
    model_shape = jax.ShapeDtypeStruct((seq_len, model_width), BF)
    terms_shape = jax.ShapeDtypeStruct((2, slots, width, width), BF)
    row_state = rows_of(state_shape.shape, tile)
    row_model = rows_of(model_shape.shape, tile)
    unit = 2 * seq_len * hidden_width * width

    cotangent_all = lax.all_gather(cotangent, "tp", axis=1, tiled=True)

    same = jnp.eye(positions, dtype=BF)
    mixer = (
        second_factor_weight.transpose(1, 0, 2)[:, :, :, None] * same[None, :, None, :]
    ).reshape(groups * positions, groups * positions)

    first_factor = w_first[0]
    first_out = dot_nn(first_factor, tokens).astype(BF)
    first_rows = lax.all_to_all(first_out, "seq", split_axis=0, concat_axis=0, tiled=True)
    mixed_part = dot_nn(mixer, first_rows).astype(BF)
    mixed = lax.all_to_all(mixed_part, "seq", split_axis=0, concat_axis=0, tiled=True)
    hidden_in = (tokens.astype(F32) + mixed.astype(F32)).astype(BF)
    hidden_all = lax.all_gather(hidden_in, "tp", axis=1, tiled=True)

    local_self = [w_self] * local
    local_cross = [w_cross] * local
    local_specs = [level_of(w_self, level) for level in range(local)]
    states = call(
        functools.partial(up_kernel, local, slots, width),
        steps,
        [block_pairs, hidden_all, w_up, *local_self, *local_cross],
        [smem, row_model, whole(w_up), *local_specs, *local_specs],
        [state_shape] * (local + 1),
        [row_state] * (local + 1),
        (local + 1) * 2 * unit,
    )
    states = list(states)
    partners = [None] * levels
    for level in range(local, levels - 1):
        partners[level] = partner_2(states[level], "tp", level - local)
        (state,) = call(
            functools.partial(across_kernel, slots, width),
            steps,
            [states[level], partners[level], w_self, w_cross],
            [row_state, row_state, level_of(w_self, level), level_of(w_cross, level)],
            [state_shape],
            [row_state],
            2 * unit,
        )
        states.append(state)
    last = levels - 1
    partners[last] = partner_2(states[last], "tp", last - local)
    down_part, grad, send = call(
        functools.partial(top_kernel, slots, width),
        steps,
        [block_pairs, states[last], partners[last], w_self, w_cross, w_down, cotangent_all],
        [
            smem,
            row_state,
            row_state,
            level_of(w_self, last),
            level_of(w_cross, last),
            whole(w_down),
            row_model,
        ],
        [model_shape, state_shape, state_shape],
        [row_model, row_state, row_state],
        7 * unit,
        [pltpu.VMEM((tile, model_width), F32)],
    )
    terms = [None] * levels

    def across_terms(level, gradient):
        (result,) = call(
            functools.partial(across_grad_kernel, slots, width),
            1,
            [states[level], partners[level], gradient],
            [whole(states[level]), whole(states[level]), whole(gradient)],
            [terms_shape],
            [whole(terms_shape)],
            2 * unit,
        )
        return lax.psum_scatter(result, "seq", scatter_dimension=2, tiled=True)

    for level in range(last, local, -1):
        incoming = partner_2(send, "tp", level - local)
        terms[level] = across_terms(level, grad)
        grad, send = call(
            functools.partial(middle_kernel, slots, width),
            steps,
            [grad, incoming, w_self, w_cross],
            [row_state, row_state, level_of(w_self, level), level_of(w_cross, level - 1)],
            [state_shape, state_shape],
            [row_state, row_state],
            2 * unit,
        )
    incoming = partner_2(send, "tp", 0)
    terms[local] = across_terms(local, grad)
    *grads, spread = call(
        functools.partial(down_kernel, local, slots, width),
        steps,
        [block_pairs, grad, incoming, w_self, w_up, *local_self, *local_cross],
        [
            smem,
            row_state,
            row_state,
            level_of(w_self, local),
            whole(w_up),
            *local_specs,
            *local_specs,
        ],
        [state_shape] * (local + 1) + [model_shape],
        [row_state] * (local + 1) + [row_model],
        (2 * local + 3) * unit,
        [pltpu.VMEM((tile, model_width), F32)],
    )
    spread_part = lax.psum_scatter(spread, "tp", scatter_dimension=1, tiled=True)
    grad_hidden = (cotangent.astype(F32) + spread_part.astype(F32)).astype(BF)
    for level in reversed(range(local)):
        (result,) = call(
            functools.partial(pair_grad_kernel, level, slots, width),
            1,
            [states[level], grads[level + 1]],
            [whole(states[level]), whole(states[level])],
            [terms_shape],
            [whole(terms_shape)],
            2 * unit,
        )
        terms[level] = lax.psum_scatter(result, "seq", scatter_dimension=2, tiled=True)

    down_sum = lax.psum_scatter(down_part, "tp", scatter_dimension=1, tiled=True)
    layer_out = (hidden_in.astype(F32) + down_sum.astype(F32)).astype(BF)

    grad_rows = lax.all_to_all(grad_hidden, "seq", split_axis=0, concat_axis=0, tiled=True)
    moved_back = dot_tn(mixer, grad_rows).astype(BF)
    returned = lax.all_to_all(moved_back, "seq", split_axis=0, concat_axis=0, tiled=True)
    cross_rows = dot_nt(grad_rows, first_rows).reshape(groups, positions, groups, positions)
    second_part = jnp.sum(cross_rows * same.astype(F32)[None, :, None, :], axis=3).transpose(1, 0, 2)
    first_part = dot_nt(returned, tokens).astype(BF)
    second_sum, first_sum = lax.psum((second_part, first_part), "tp")
    grad_mix = dot_tn(first_factor, returned)
    grad_tokens = (grad_hidden.astype(F32) + grad_mix).astype(BF)
    level_terms = jnp.stack(terms, axis=1).astype(F32) * token_scale
    return (
        layer_out,
        grad_tokens,
        (first_sum.astype(F32) * model_width_scale)[None],
        second_sum * model_width_scale,
        level_terms[0],
        level_terms[1],
    )


def solution(mesh):
    in_specs = (
        P("seq", "tp"),
        P("seq", None, None),
        P("seq", None, None),
        P("tp", None, None, None),
        P(None, "tp", None, None),
        P(None, "tp", None, None),
        P("tp", None, None, None),
        P("tp", None),
        P("seq", "tp"),
    )
    out_specs = (
        P("seq", "tp"),
        P("seq", "tp"),
        P("seq", None, None),
        P("seq", None, None),
        P(None, "tp", "seq", None),
        P(None, "tp", "seq", None),
    )
    return jax.shard_map(
        per_device, mesh=mesh, in_specs=in_specs, out_specs=out_specs, check_vma=False
    )
```

```python
import functools
import math

import jax
import jax.numpy as jnp
from jax import lax
from jax.experimental import pallas as pl
from jax.experimental.pallas import tpu as pltpu
from jax.sharding import PartitionSpec as P

BF = jnp.bfloat16
F32 = jnp.float32
VMEM_BYTES = 56 * 1024 * 1024
UNROLL = 4


def dot(left, right, contract):
    return lax.dot_general(left, right, (contract, ((), ())), preferred_element_type=F32)


def dot_nn(left, right):
    return dot(left, right, ((1,), (0,)))


def dot_nt(left, right):
    return dot(left, right, ((1,), (1,)))


def dot_tn(left, right):
    return dot(left, right, ((0,), (0,)))


def partner_2(value, axis, bit):
    mask = 2**bit
    pairs = [(source, source ^ mask) for source in range(lax.axis_size(axis))]
    return lax.ppermute(value, axis, pairs)


def bit_of(axis, bit):
    return (lax.axis_index(axis) // 2**bit) % 2


def bits_of(axis):
    return lax.axis_size(axis).bit_length() - 1


def halved_sum(value, axis, dim):
    for bit in range(bits_of(axis)):
        shape = value.shape
        folded = value.reshape(shape[:dim] + (shape[dim] // 2, 2) + shape[dim + 1 :])
        mine = bit_of(axis, bit)
        keep = lax.dynamic_index_in_dim(folded, mine, dim + 1, keepdims=False)
        give = lax.dynamic_index_in_dim(folded, 1 - mine, dim + 1, keepdims=False)
        total = keep.astype(F32) + partner_2(give, axis, bit).astype(F32)
        value = total.astype(BF)
    return lax.squeeze(total, (dim,))


def doubled_gather(value, axis):
    shape = value.shape
    count = 0
    for bit in reversed(range(bits_of(axis))):
        other = partner_2(value, axis, bit)
        low = bit_of(axis, bit) == 0
        value = jnp.stack(
            [jnp.where(low, value, other), jnp.where(low, other, value)], axis=count
        )
        count += 1
    return value.reshape((lax.axis_size(axis),) + shape)


def exchanged_sum(value, axis):
    kind = value.dtype
    for bit in range(bits_of(axis)):
        total = value.astype(F32) + partner_2(value, axis, bit).astype(F32)
        value = total.astype(kind)
    return total


def lanes(index, width):
    return pl.ds(pl.multiple_of(index * width, width), width)


def pair_of(index, level):
    low = 2**level
    first = (index // low) * (2 * low) + index % low
    return first, first + low


def pair_matrix(w_self, w_cross, first, second):
    top = jnp.concatenate([w_self[0, first], w_cross[0, second]], axis=1)
    bottom = jnp.concatenate([w_cross[0, first], w_self[0, second]], axis=1)
    return jnp.concatenate([top, bottom], axis=0)


def side_by_side(ref, first, second, width):
    return jnp.concatenate([ref[:, lanes(first, width)], ref[:, lanes(second, width)]], axis=1)


def blocks_of(ref, first, second, width):
    per = ref.shape[2] // width
    return jnp.concatenate(
        [ref[i // per, :, lanes(lax.rem(i, per), width)] for i in (first, second)], axis=1
    )


def put_chunks(out, total):
    count, _, size = out.shape
    for chunk in range(count):
        out[chunk] = total[:, chunk * size : (chunk + 1) * size].astype(BF)


def up_kernel(levels, slots, width, pairs, hidden, w_up, *refs):
    w_self, w_cross, states = refs[:levels], refs[levels : 2 * levels], refs[2 * levels :]

    @pl.loop(0, slots, unroll=UNROLL)
    def _(j):
        both = blocks_of(hidden, pairs[j, 0], pairs[j, 1], width)
        matrix = jnp.concatenate([w_up[j, 0], w_up[j, 1]], axis=0)
        states[0][:, lanes(j, width)] = dot_nn(both, matrix).astype(BF)

    for level in range(levels):

        @pl.loop(0, slots // 2, unroll=UNROLL)
        def _(index):
            first, second = pair_of(index, level)
            both = side_by_side(states[level], first, second, width)
            result = dot_nn(both, pair_matrix(w_self[level], w_cross[level], first, second)).astype(BF)
            states[level + 1][:, lanes(first, width)] = result[:, :width]
            states[level + 1][:, lanes(second, width)] = result[:, width:]


def across_kernel(slots, width, state, partner, w_self, w_cross, out):
    @pl.loop(0, slots, unroll=UNROLL)
    def _(j):
        both = jnp.concatenate([state[:, lanes(j, width)], partner[:, lanes(j, width)]], axis=1)
        matrix = jnp.concatenate([w_self[0, j], w_cross[0, j]], axis=0)
        out[:, lanes(j, width)] = dot_nn(both, matrix).astype(BF)


def top_kernel(
    slots, width, pairs, state, partner, w_self, w_cross, w_down, cotangent, down, grad, send, total
):
    total[...] = jnp.zeros_like(total)

    @pl.loop(0, slots, unroll=UNROLL)
    def _(j):
        first, second = pairs[j, 0], pairs[j, 1]
        both = jnp.concatenate([state[:, lanes(j, width)], partner[:, lanes(j, width)]], axis=1)
        matrix = jnp.concatenate([w_self[0, j], w_cross[0, j]], axis=0)
        top = dot_nn(both, matrix).astype(BF).astype(F32)
        root = math.sqrt(2.0 / math.pi)
        square = top * top
        bend = jnp.tanh(root * (top + 0.044715 * (square * top)))
        active = (0.5 * top * (1.0 + bend)).astype(BF)
        slope = 0.5 * (1.0 + bend) + 0.5 * top * (1.0 - bend * bend) * (
            root * (1.0 + (3 * 0.044715) * square)
        )
        w_both = jnp.concatenate([w_down[j, 0], w_down[j, 1]], axis=1)
        pieces = dot_nn(active, w_both)
        total[:, lanes(first, width)] += pieces[:, :width]
        total[:, lanes(second, width)] += pieces[:, width:]
        grad_act = dot_nt(blocks_of(cotangent, first, second, width), w_both)
        grad_top = (grad_act * slope).astype(BF)
        grad[:, lanes(j, width)] = grad_top
        send[:, lanes(j, width)] = dot_nt(grad_top, w_cross[0, j]).astype(BF)

    put_chunks(down, total)


def across_grad_kernel(slots, width, state, partner, grad, terms):
    @pl.loop(0, slots, unroll=UNROLL)
    def _(j):
        both = jnp.concatenate([state[:, lanes(j, width)], partner[:, lanes(j, width)]], axis=1)
        result = dot_tn(both, grad[:, lanes(j, width)]).astype(BF)
        terms[0, 0, j] = result[:width]
        terms[0, 1, j] = result[width:]


def middle_kernel(slots, width, grad, incoming, w_self, w_cross_below, out, send):
    @pl.loop(0, slots, unroll=UNROLL)
    def _(j):
        own = dot_nt(grad[:, lanes(j, width)], w_self[0, j])
        result = (own + incoming[:, lanes(j, width)].astype(F32)).astype(BF)
        out[:, lanes(j, width)] = result
        send[:, lanes(j, width)] = dot_nt(result, w_cross_below[0, j]).astype(BF)


def down_kernel(levels, slots, width, pairs, grad, incoming, w_self_above, w_up, *refs):
    w_self, w_cross = refs[:levels], refs[levels : 2 * levels]
    grads = refs[2 * levels : 3 * levels + 1]
    spread, total = refs[3 * levels + 1 :]

    @pl.loop(0, slots, unroll=UNROLL)
    def _(j):
        own = dot_nt(grad[:, lanes(j, width)], w_self_above[0, j])
        result = own + incoming[:, lanes(j, width)].astype(F32)
        grads[levels][:, lanes(j, width)] = result.astype(BF)

    for level in reversed(range(levels)):

        @pl.loop(0, slots // 2, unroll=UNROLL)
        def _(index):
            first, second = pair_of(index, level)
            both = side_by_side(grads[level + 1], first, second, width)
            result = dot_nt(both, pair_matrix(w_self[level], w_cross[level], first, second)).astype(BF)
            grads[level][:, lanes(first, width)] = result[:, :width]
            grads[level][:, lanes(second, width)] = result[:, width:]

    total[...] = jnp.zeros_like(total)

    @pl.loop(0, slots, unroll=UNROLL)
    def _(j):
        matrix = jnp.concatenate([w_up[j, 0], w_up[j, 1]], axis=0)
        pieces = dot_nt(grads[0][:, lanes(j, width)], matrix)
        total[:, lanes(pairs[j, 0], width)] += pieces[:, :width]
        total[:, lanes(pairs[j, 1], width)] += pieces[:, width:]

    put_chunks(spread, total)


def pair_grad_kernel(group, slots, width, *refs):
    count = len(group)
    states, grads, terms = refs[:count], refs[count : 2 * count], refs[2 * count]
    for at, level in enumerate(group):

        @pl.loop(0, slots // 2, unroll=UNROLL)
        def _(index):
            first, second = pair_of(index, level)
            result = dot_tn(
                side_by_side(states[at], first, second, width),
                side_by_side(grads[at], first, second, width),
            ).astype(BF)
            terms[at, 0, first] = result[:width, :width]
            terms[at, 1, second] = result[:width, width:]
            terms[at, 1, first] = result[width:, :width]
            terms[at, 0, second] = result[width:, width:]


def whole(array):
    return pl.BlockSpec(array.shape, lambda i: (0,) * array.ndim)


def level_of(array, level):
    return pl.BlockSpec((1,) + array.shape[1:], lambda i: (level, 0, 0, 0))


def rows_of(shape, tile):
    return pl.BlockSpec((tile, shape[1]), lambda i: (i, 0))


def chunk_rows_of(shape, tile):
    return pl.BlockSpec((shape[0], tile, shape[2]), lambda i: (0, i, 0))


def call(kernel, steps, operands, in_specs, out_shapes, out_specs, flops, scratch=()):
    moved = sum(x.size * x.dtype.itemsize for x in operands[:4])
    moved += sum(math.prod(x.shape) * x.dtype.itemsize for x in out_shapes)
    return pl.pallas_call(
        kernel,
        grid=(steps,),
        in_specs=in_specs,
        out_specs=out_specs,
        out_shape=out_shapes,
        scratch_shapes=scratch,
        compiler_params=pltpu.CompilerParams(vmem_limit_bytes=VMEM_BYTES),
        cost_estimate=pl.CostEstimate(flops=flops, bytes_accessed=moved, transcendentals=0),
    )(*operands)


def per_device(
    tokens, w_first, second_factor_weight, w_up, w_self, w_cross, w_down, block_pairs, cotangent
):
    seq_len, width_local = tokens.shape
    levels, slots, width, _ = w_self.shape
    model_width = width_local * lax.axis_size("tp")
    local = slots.bit_length() - 1
    hidden_width = slots * width
    total_tokens = seq_len * lax.axis_size("seq")
    token_scale = 1.0 / math.sqrt(total_tokens)
    model_width_scale = 1.0 / math.sqrt(model_width)
    positions, groups, _ = second_factor_weight.shape
    tile = seq_len // 2
    steps = 2
    smem = pl.BlockSpec(memory_space=pltpu.SMEM)
    state_shape = jax.ShapeDtypeStruct((seq_len, hidden_width), BF)
    model_shape = jax.ShapeDtypeStruct((lax.axis_size("tp"), seq_len, width_local), BF)
    seq_size = lax.axis_size("seq")

    def terms_of(count):
        return jax.ShapeDtypeStruct((count, 2, slots, width, width), BF)

    def summed(result):
        chunked = result.reshape(result.shape[:3] + (seq_size, width // seq_size, width))
        return halved_sum(chunked, "seq", 3)

    row_state = rows_of(state_shape.shape, tile)
    row_model = chunk_rows_of(model_shape.shape, tile)
    unit = 2 * seq_len * hidden_width * width

    cotangent_all = doubled_gather(cotangent, "tp")

    same = jnp.eye(positions, dtype=BF)
    mixer = (
        second_factor_weight.transpose(1, 0, 2)[:, :, :, None] * same[None, :, None, :]
    ).reshape(groups * positions, groups * positions)

    first_factor = w_first[0]
    first_out = dot_nn(first_factor, tokens).astype(BF)
    first_rows = lax.all_to_all(first_out, "seq", split_axis=0, concat_axis=0, tiled=True)
    mixed_part = dot_nn(mixer, first_rows).astype(BF)
    mixed = lax.all_to_all(mixed_part, "seq", split_axis=0, concat_axis=0, tiled=True)
    hidden_in = (tokens.astype(F32) + mixed.astype(F32)).astype(BF)
    hidden_all = doubled_gather(hidden_in, "tp")

    local_self = [w_self] * local
    local_cross = [w_cross] * local
    local_specs = [level_of(w_self, level) for level in range(local)]
    states = call(
        functools.partial(up_kernel, local, slots, width),
        steps,
        [block_pairs, hidden_all, w_up, *local_self, *local_cross],
        [smem, row_model, whole(w_up), *local_specs, *local_specs],
        [state_shape] * (local + 1),
        [row_state] * (local + 1),
        (local + 1) * 2 * unit,
    )
    states = list(states)
    partners = [None] * levels
    for level in range(local, levels - 1):
        partners[level] = partner_2(states[level], "tp", level - local)
        (state,) = call(
            functools.partial(across_kernel, slots, width),
            steps,
            [states[level], partners[level], w_self, w_cross],
            [row_state, row_state, level_of(w_self, level), level_of(w_cross, level)],
            [state_shape],
            [row_state],
            2 * unit,
        )
        states.append(state)
    last = levels - 1
    partners[last] = partner_2(states[last], "tp", last - local)
    down_part, grad, send = call(
        functools.partial(top_kernel, slots, width),
        steps,
        [block_pairs, states[last], partners[last], w_self, w_cross, w_down, cotangent_all],
        [
            smem,
            row_state,
            row_state,
            level_of(w_self, last),
            level_of(w_cross, last),
            whole(w_down),
            row_model,
        ],
        [model_shape, state_shape, state_shape],
        [row_model, row_state, row_state],
        7 * unit,
        [pltpu.VMEM((tile, model_width), F32)],
    )
    terms = [None] * levels

    def across_terms(level, gradient):
        (result,) = call(
            functools.partial(across_grad_kernel, slots, width),
            1,
            [states[level], partners[level], gradient],
            [whole(states[level]), whole(states[level]), whole(gradient)],
            [terms_of(1)],
            [whole(terms_of(1))],
            2 * unit,
        )
        return summed(result)[0]

    for level in range(last, local, -1):
        incoming = partner_2(send, "tp", level - local)
        terms[level] = across_terms(level, grad)
        grad, send = call(
            functools.partial(middle_kernel, slots, width),
            steps,
            [grad, incoming, w_self, w_cross],
            [row_state, row_state, level_of(w_self, level), level_of(w_cross, level - 1)],
            [state_shape, state_shape],
            [row_state, row_state],
            2 * unit,
        )
    incoming = partner_2(send, "tp", 0)
    terms[local] = across_terms(local, grad)
    *grads, spread = call(
        functools.partial(down_kernel, local, slots, width),
        steps,
        [block_pairs, grad, incoming, w_self, w_up, *local_self, *local_cross],
        [
            smem,
            row_state,
            row_state,
            level_of(w_self, local),
            whole(w_up),
            *local_specs,
            *local_specs,
        ],
        [state_shape] * (local + 1) + [model_shape],
        [row_state] * (local + 1) + [row_model],
        (2 * local + 3) * unit,
        [pltpu.VMEM((tile, model_width), F32)],
    )
    spread_part = halved_sum(spread, "tp", 0)
    grad_hidden = (cotangent.astype(F32) + spread_part).astype(BF)
    for top in range(local, 0, -2):
        group = list(range(max(top - 2, 0), top))
        (result,) = call(
            functools.partial(pair_grad_kernel, group, slots, width),
            1,
            [states[level] for level in group] + [grads[level + 1] for level in group],
            [whole(states[0])] * (2 * len(group)),
            [terms_of(len(group))],
            [whole(terms_of(len(group)))],
            2 * len(group) * unit,
        )
        sums = summed(result)
        for at, level in enumerate(group):
            terms[level] = sums[at]

    down_sum = halved_sum(down_part, "tp", 0)
    layer_out = (hidden_in.astype(F32) + down_sum).astype(BF)

    grad_rows = lax.all_to_all(grad_hidden, "seq", split_axis=0, concat_axis=0, tiled=True)
    moved_back = dot_tn(mixer, grad_rows).astype(BF)
    returned = lax.all_to_all(moved_back, "seq", split_axis=0, concat_axis=0, tiled=True)
    cross_rows = dot_nt(grad_rows, first_rows).reshape(groups, positions, groups, positions)
    second_part = jnp.sum(cross_rows * same.astype(F32)[None, :, None, :], axis=3).transpose(1, 0, 2)
    first_part = dot_nt(returned, tokens).astype(BF)
    second_sum = exchanged_sum(second_part, "tp")
    first_sum = exchanged_sum(first_part, "tp")
    grad_mix = dot_tn(first_factor, returned)
    grad_tokens = (grad_hidden.astype(F32) + grad_mix).astype(BF)
    level_terms = jnp.stack(terms, axis=1) * token_scale
    return (
        layer_out,
        grad_tokens,
        (first_sum * model_width_scale)[None],
        second_sum * model_width_scale,
        level_terms[0],
        level_terms[1],
    )


def solution(mesh):
    in_specs = (
        P("seq", "tp"),
        P("seq", None, None),
        P("seq", None, None),
        P("tp", None, None, None),
        P(None, "tp", None, None),
        P(None, "tp", None, None),
        P("tp", None, None, None),
        P("tp", None),
        P("seq", "tp"),
    )
    out_specs = (
        P("seq", "tp"),
        P("seq", "tp"),
        P("seq", None, None),
        P("seq", None, None),
        P(None, "tp", "seq", None),
        P(None, "tp", "seq", None),
    )
    return jax.shard_map(
        per_device, mesh=mesh, in_specs=in_specs, out_specs=out_specs, check_vma=False
    )
```

```python
import functools
import math

import jax
import jax.numpy as jnp
from jax import lax
from jax.experimental import pallas as pl
from jax.experimental.pallas import tpu as pltpu
from jax.sharding import PartitionSpec as P

BF = jnp.bfloat16
F32 = jnp.float32
VMEM_BYTES = 56 * 1024 * 1024
UNROLL = 4


def dot(left, right, contract):
    return lax.dot_general(left, right, (contract, ((), ())), preferred_element_type=F32)


def dot_nn(left, right):
    return dot(left, right, ((1,), (0,)))


def dot_nt(left, right):
    return dot(left, right, ((1,), (1,)))


def dot_tn(left, right):
    return dot(left, right, ((0,), (0,)))


def partner_2(value, axis, bit):
    mask = 2**bit
    pairs = [(source, source ^ mask) for source in range(lax.axis_size(axis))]
    return lax.ppermute(value, axis, pairs)


def bit_of(axis, bit):
    return (lax.axis_index(axis) // 2**bit) % 2


def bits_of(axis):
    return lax.axis_size(axis).bit_length() - 1


def halve(value, axis, dim, left, bit):
    at = dim + left.index(bit)
    mine = bit_of(axis, bit)
    keep = lax.dynamic_index_in_dim(value, mine, at, keepdims=False)
    give = lax.dynamic_index_in_dim(value, 1 - mine, at, keepdims=False)
    total = keep.astype(F32) + partner_2(give, axis, bit).astype(F32)
    return total, [other for other in left if other != bit]


def halved_sum(value, axis, dim, order):
    left = list(reversed(range(bits_of(axis))))
    shape = value.shape
    value = value.reshape(shape[:dim] + (2,) * len(left) + shape[dim + 1 :])
    steps = []
    for bit in order:
        total, left = halve(value, axis, dim, left, bit)
        value = total.astype(BF)
        steps.append(value)
    return total, steps[0]


def doubled_gather(value, axis):
    shape = value.shape
    count = 0
    for bit in reversed(range(bits_of(axis))):
        other = partner_2(value, axis, bit)
        low = bit_of(axis, bit) == 0
        value = jnp.stack(
            [jnp.where(low, value, other), jnp.where(low, other, value)], axis=count
        )
        count += 1
    return value.reshape((lax.axis_size(axis),) + shape)


def exchanged_sum(value, axis):
    kind = value.dtype
    for bit in range(bits_of(axis)):
        total = value.astype(F32) + partner_2(value, axis, bit).astype(F32)
        value = total.astype(kind)
    return total


def lanes(index, width):
    return pl.ds(pl.multiple_of(index * width, width), width)


def pair_of(index, level):
    low = 2**level
    first = (index // low) * (2 * low) + index % low
    return first, first + low


def pair_matrix(w_self, w_cross, first, second):
    top = jnp.concatenate([w_self[0, first], w_cross[0, second]], axis=1)
    bottom = jnp.concatenate([w_cross[0, first], w_self[0, second]], axis=1)
    return jnp.concatenate([top, bottom], axis=0)


def side_by_side(ref, first, second, width):
    return jnp.concatenate([ref[:, lanes(first, width)], ref[:, lanes(second, width)]], axis=1)


def blocks_of(ref, first, second, width):
    per = ref.shape[2] // width
    return jnp.concatenate(
        [ref[i // per, :, lanes(lax.rem(i, per), width)] for i in (first, second)], axis=1
    )


def put_chunks(out, total):
    count, _, size = out.shape
    for chunk in range(count):
        out[chunk] = total[:, chunk * size : (chunk + 1) * size].astype(BF)


def up_kernel(levels, slots, width, pairs, hidden, w_up, *refs):
    w_self, w_cross, states = refs[:levels], refs[levels : 2 * levels], refs[2 * levels :]

    @pl.loop(0, slots, unroll=UNROLL)
    def _(j):
        both = blocks_of(hidden, pairs[j, 0], pairs[j, 1], width)
        matrix = jnp.concatenate([w_up[j, 0], w_up[j, 1]], axis=0)
        states[0][:, lanes(j, width)] = dot_nn(both, matrix).astype(BF)

    for level in range(levels):

        @pl.loop(0, slots // 2, unroll=UNROLL)
        def _(index):
            first, second = pair_of(index, level)
            both = side_by_side(states[level], first, second, width)
            result = dot_nn(both, pair_matrix(w_self[level], w_cross[level], first, second)).astype(BF)
            states[level + 1][:, lanes(first, width)] = result[:, :width]
            states[level + 1][:, lanes(second, width)] = result[:, width:]


def across_kernel(slots, width, state, partner, w_self, w_cross, out):
    @pl.loop(0, slots, unroll=UNROLL)
    def _(j):
        both = jnp.concatenate([state[:, lanes(j, width)], partner[:, lanes(j, width)]], axis=1)
        matrix = jnp.concatenate([w_self[0, j], w_cross[0, j]], axis=0)
        out[:, lanes(j, width)] = dot_nn(both, matrix).astype(BF)


def top_kernel(
    slots, width, pairs, state, partner, w_self, w_cross, w_down, cotangent, down, grad, send, total
):
    total[...] = jnp.zeros_like(total)

    @pl.loop(0, slots, unroll=UNROLL)
    def _(j):
        first, second = pairs[j, 0], pairs[j, 1]
        both = jnp.concatenate([state[:, lanes(j, width)], partner[:, lanes(j, width)]], axis=1)
        matrix = jnp.concatenate([w_self[0, j], w_cross[0, j]], axis=0)
        top = dot_nn(both, matrix).astype(BF).astype(F32)
        root = math.sqrt(2.0 / math.pi)
        square = top * top
        bend = jnp.tanh(root * (top + 0.044715 * (square * top)))
        active = (0.5 * top * (1.0 + bend)).astype(BF)
        slope = 0.5 * (1.0 + bend) + 0.5 * top * (1.0 - bend * bend) * (
            root * (1.0 + (3 * 0.044715) * square)
        )
        w_both = jnp.concatenate([w_down[j, 0], w_down[j, 1]], axis=1)
        pieces = dot_nn(active, w_both)
        total[:, lanes(first, width)] += pieces[:, :width]
        total[:, lanes(second, width)] += pieces[:, width:]
        grad_act = dot_nt(blocks_of(cotangent, first, second, width), w_both)
        grad_top = (grad_act * slope).astype(BF)
        grad[:, lanes(j, width)] = grad_top
        send[:, lanes(j, width)] = dot_nt(grad_top, w_cross[0, j]).astype(BF)

    put_chunks(down, total)


def across_grad_kernel(slots, width, state, partner, grad, after, terms):
    @pl.loop(0, slots, unroll=UNROLL)
    def _(j):
        both = jnp.concatenate([state[:, lanes(j, width)], partner[:, lanes(j, width)]], axis=1)
        result = dot_tn(both, grad[:, lanes(j, width)]).astype(BF)
        terms[0, 0, j] = result[:width]
        terms[0, 1, j] = result[width:]


def middle_kernel(slots, width, grad, incoming, w_self, w_cross_below, out, send):
    @pl.loop(0, slots, unroll=UNROLL)
    def _(j):
        own = dot_nt(grad[:, lanes(j, width)], w_self[0, j])
        result = (own + incoming[:, lanes(j, width)].astype(F32)).astype(BF)
        out[:, lanes(j, width)] = result
        send[:, lanes(j, width)] = dot_nt(result, w_cross_below[0, j]).astype(BF)


def down_kernel(levels, slots, width, pairs, grad, incoming, w_self_above, w_up, *refs):
    w_self, w_cross = refs[:levels], refs[levels : 2 * levels]
    grads = refs[2 * levels : 3 * levels + 1]
    spread, total = refs[3 * levels + 1 :]

    @pl.loop(0, slots, unroll=UNROLL)
    def _(j):
        own = dot_nt(grad[:, lanes(j, width)], w_self_above[0, j])
        result = own + incoming[:, lanes(j, width)].astype(F32)
        grads[levels][:, lanes(j, width)] = result.astype(BF)

    for level in reversed(range(levels)):

        @pl.loop(0, slots // 2, unroll=UNROLL)
        def _(index):
            first, second = pair_of(index, level)
            both = side_by_side(grads[level + 1], first, second, width)
            result = dot_nt(both, pair_matrix(w_self[level], w_cross[level], first, second)).astype(BF)
            grads[level][:, lanes(first, width)] = result[:, :width]
            grads[level][:, lanes(second, width)] = result[:, width:]

    total[...] = jnp.zeros_like(total)

    @pl.loop(0, slots, unroll=UNROLL)
    def _(j):
        matrix = jnp.concatenate([w_up[j, 0], w_up[j, 1]], axis=0)
        pieces = dot_nt(grads[0][:, lanes(j, width)], matrix)
        total[:, lanes(pairs[j, 0], width)] += pieces[:, :width]
        total[:, lanes(pairs[j, 1], width)] += pieces[:, width:]

    put_chunks(spread, total)


def pair_grad_kernel(group, slots, width, *refs):
    count = len(group)
    states, grads, terms = refs[:count], refs[count : 2 * count], refs[2 * count + 1]
    for at, level in enumerate(group):

        @pl.loop(0, slots // 2, unroll=UNROLL)
        def _(index):
            first, second = pair_of(index, level)
            result = dot_tn(
                side_by_side(states[at], first, second, width),
                side_by_side(grads[at], first, second, width),
            ).astype(BF)
            terms[at, 0, first] = result[:width, :width]
            terms[at, 1, second] = result[:width, width:]
            terms[at, 1, first] = result[width:, :width]
            terms[at, 0, second] = result[width:, width:]


def whole(array):
    return pl.BlockSpec(array.shape, lambda i: (0,) * array.ndim)


def level_of(array, level):
    return pl.BlockSpec((1,) + array.shape[1:], lambda i: (level, 0, 0, 0))


def rows_of(shape, tile):
    return pl.BlockSpec((tile, shape[1]), lambda i: (i, 0))


def chunk_rows_of(shape, tile):
    return pl.BlockSpec((shape[0], tile, shape[2]), lambda i: (0, i, 0))


def call(kernel, steps, operands, in_specs, out_shapes, out_specs, flops, scratch=()):
    moved = sum(x.size * x.dtype.itemsize for x in operands[:4])
    moved += sum(math.prod(x.shape) * x.dtype.itemsize for x in out_shapes)
    return pl.pallas_call(
        kernel,
        grid=(steps,),
        in_specs=in_specs,
        out_specs=out_specs,
        out_shape=out_shapes,
        scratch_shapes=scratch,
        compiler_params=pltpu.CompilerParams(vmem_limit_bytes=VMEM_BYTES),
        cost_estimate=pl.CostEstimate(flops=flops, bytes_accessed=moved, transcendentals=0),
    )(*operands)


def per_device(
    tokens, w_first, second_factor_weight, w_up, w_self, w_cross, w_down, block_pairs, cotangent
):
    seq_len, width_local = tokens.shape
    levels, slots, width, _ = w_self.shape
    model_width = width_local * lax.axis_size("tp")
    local = slots.bit_length() - 1
    hidden_width = slots * width
    total_tokens = seq_len * lax.axis_size("seq")
    token_scale = 1.0 / math.sqrt(total_tokens)
    model_width_scale = 1.0 / math.sqrt(model_width)
    positions, groups, _ = second_factor_weight.shape
    tile = seq_len // 2
    steps = 2
    smem = pl.BlockSpec(memory_space=pltpu.SMEM)
    state_shape = jax.ShapeDtypeStruct((seq_len, hidden_width), BF)
    model_shape = jax.ShapeDtypeStruct((lax.axis_size("tp"), seq_len, width_local), BF)
    seq_size = lax.axis_size("seq")

    def terms_of(count):
        return jax.ShapeDtypeStruct((count, 2, slots, width, width), BF)

    seq_bits = list(range(bits_of("seq")))
    orders = [seq_bits, seq_bits[1:2] + seq_bits[:1] + seq_bits[2:]]
    tp_bits = list(range(bits_of("tp")))

    def summed(result, order):
        chunked = result.reshape(result.shape[:3] + (seq_size, width // seq_size, width))
        return halved_sum(chunked, "seq", 3, order)[0]

    row_state = rows_of(state_shape.shape, tile)
    row_model = chunk_rows_of(model_shape.shape, tile)
    unit = 2 * seq_len * hidden_width * width

    cotangent_all = doubled_gather(cotangent, "tp")

    same = jnp.eye(positions, dtype=BF)
    mixer = (
        second_factor_weight.transpose(1, 0, 2)[:, :, :, None] * same[None, :, None, :]
    ).reshape(groups * positions, groups * positions)

    first_factor = w_first[0]
    first_out = dot_nn(first_factor, tokens).astype(BF)
    first_rows = lax.all_to_all(first_out, "seq", split_axis=0, concat_axis=0, tiled=True)
    mixed_part = dot_nn(mixer, first_rows).astype(BF)
    mixed = lax.all_to_all(mixed_part, "seq", split_axis=0, concat_axis=0, tiled=True)
    hidden_in = (tokens.astype(F32) + mixed.astype(F32)).astype(BF)
    hidden_all = doubled_gather(hidden_in, "tp")

    local_self = [w_self] * local
    local_cross = [w_cross] * local
    local_specs = [level_of(w_self, level) for level in range(local)]
    states = call(
        functools.partial(up_kernel, local, slots, width),
        steps,
        [block_pairs, hidden_all, w_up, *local_self, *local_cross],
        [smem, row_model, whole(w_up), *local_specs, *local_specs],
        [state_shape] * (local + 1),
        [row_state] * (local + 1),
        (local + 1) * 2 * unit,
    )
    states = list(states)
    partners = [None] * levels
    for level in range(local, levels - 1):
        partners[level] = partner_2(states[level], "tp", level - local)
        (state,) = call(
            functools.partial(across_kernel, slots, width),
            steps,
            [states[level], partners[level], w_self, w_cross],
            [row_state, row_state, level_of(w_self, level), level_of(w_cross, level)],
            [state_shape],
            [row_state],
            2 * unit,
        )
        states.append(state)
    last = levels - 1
    partners[last] = partner_2(states[last], "tp", last - local)
    down_part, grad, send = call(
        functools.partial(top_kernel, slots, width),
        steps,
        [block_pairs, states[last], partners[last], w_self, w_cross, w_down, cotangent_all],
        [
            smem,
            row_state,
            row_state,
            level_of(w_self, last),
            level_of(w_cross, last),
            whole(w_down),
            row_model,
        ],
        [model_shape, state_shape, state_shape],
        [row_model, row_state, row_state],
        7 * unit,
        [pltpu.VMEM((tile, model_width), F32)],
    )
    terms = [None] * levels

    anywhere = pl.BlockSpec(memory_space=pl.ANY)

    def across_terms(level, gradient, after):
        (result,) = call(
            functools.partial(across_grad_kernel, slots, width),
            1,
            [states[level], partners[level], gradient, after],
            [whole(states[level]), whole(states[level]), whole(gradient), anywhere],
            [terms_of(1)],
            [whole(terms_of(1))],
            2 * unit,
        )
        return summed(result, orders[level % 2])[0]

    for level in range(last, local, -1):
        incoming = partner_2(send, "tp", level - local)
        terms[level] = across_terms(level, grad, send)
        grad, send = call(
            functools.partial(middle_kernel, slots, width),
            steps,
            [grad, incoming, w_self, w_cross],
            [row_state, row_state, level_of(w_self, level), level_of(w_cross, level - 1)],
            [state_shape, state_shape],
            [row_state, row_state],
            2 * unit,
        )
    incoming = partner_2(send, "tp", 0)
    grad_above = grad
    *grads, spread = call(
        functools.partial(down_kernel, local, slots, width),
        steps,
        [block_pairs, grad, incoming, w_self, w_up, *local_self, *local_cross],
        [
            smem,
            row_state,
            row_state,
            level_of(w_self, local),
            whole(w_up),
            *local_specs,
            *local_specs,
        ],
        [state_shape] * (local + 1) + [model_shape],
        [row_state] * (local + 1) + [row_model],
        (2 * local + 3) * unit,
        [pltpu.VMEM((tile, model_width), F32)],
    )
    spread_part, spread_first = halved_sum(spread, "tp", 0, tp_bits)
    terms[local] = across_terms(local, grad_above, spread)
    grad_hidden = (cotangent.astype(F32) + spread_part).astype(BF)
    for top in range(local, 0, -2):
        group = list(range(max(top - 2, 0), top))
        (result,) = call(
            functools.partial(pair_grad_kernel, group, slots, width),
            1,
            [states[level] for level in group]
            + [grads[level + 1] for level in group]
            + [spread_first],
            [whole(states[0])] * (2 * len(group)) + [anywhere],
            [terms_of(len(group))],
            [whole(terms_of(len(group)))],
            2 * len(group) * unit,
        )
        sums = summed(result, orders[(local - top) // 2 % 2])
        for at, level in enumerate(group):
            terms[level] = sums[at]

    down_sum, _ = halved_sum(down_part, "tp", 0, tp_bits)
    layer_out = (hidden_in.astype(F32) + down_sum).astype(BF)

    grad_rows = lax.all_to_all(grad_hidden, "seq", split_axis=0, concat_axis=0, tiled=True)
    moved_back = dot_tn(mixer, grad_rows).astype(BF)
    returned = lax.all_to_all(moved_back, "seq", split_axis=0, concat_axis=0, tiled=True)
    cross_rows = dot_nt(grad_rows, first_rows).reshape(groups, positions, groups, positions)
    second_part = jnp.sum(cross_rows * same.astype(F32)[None, :, None, :], axis=3).transpose(1, 0, 2)
    first_part = dot_nt(returned, tokens).astype(BF)
    second_sum = exchanged_sum(second_part, "tp")
    first_sum = exchanged_sum(first_part, "tp")
    grad_mix = dot_tn(first_factor, returned)
    grad_tokens = (grad_hidden.astype(F32) + grad_mix).astype(BF)
    level_terms = jnp.stack(terms, axis=1) * token_scale
    return (
        layer_out,
        grad_tokens,
        (first_sum * model_width_scale)[None],
        second_sum * model_width_scale,
        level_terms[0],
        level_terms[1],
    )


def solution(mesh):
    in_specs = (
        P("seq", "tp"),
        P("seq", None, None),
        P("seq", None, None),
        P("tp", None, None, None),
        P(None, "tp", None, None),
        P(None, "tp", None, None),
        P("tp", None, None, None),
        P("tp", None),
        P("seq", "tp"),
    )
    out_specs = (
        P("seq", "tp"),
        P("seq", "tp"),
        P("seq", None, None),
        P("seq", None, None),
        P(None, "tp", "seq", None),
        P(None, "tp", "seq", None),
    )
    return jax.shard_map(
        per_device, mesh=mesh, in_specs=in_specs, out_specs=out_specs, check_vma=False
    )
```

```python
import functools
import math

import jax
import jax.numpy as jnp
from jax import lax
from jax.experimental import pallas as pl
from jax.experimental.pallas import tpu as pltpu
from jax.sharding import PartitionSpec as P

BF = jnp.bfloat16
F32 = jnp.float32
VMEM_BYTES = 56 * 1024 * 1024
UNROLL = 4


def dot(left, right, contract):
    return lax.dot_general(left, right, (contract, ((), ())), preferred_element_type=F32)


def dot_nn(left, right):
    return dot(left, right, ((1,), (0,)))


def dot_nt(left, right):
    return dot(left, right, ((1,), (1,)))


def dot_tn(left, right):
    return dot(left, right, ((0,), (0,)))


def partner_2(value, axis, bit):
    mask = 2**bit
    pairs = [(source, source ^ mask) for source in range(lax.axis_size(axis))]
    return lax.ppermute(value, axis, pairs)


def bit_of(axis, bit):
    return (lax.axis_index(axis) // 2**bit) % 2


def bits_of(axis):
    return lax.axis_size(axis).bit_length() - 1


def nothing(value, tie, out):
    pass


def hold(value, tie):
    anywhere = pl.BlockSpec(memory_space=pl.ANY)
    return pl.pallas_call(
        nothing,
        out_shape=jax.ShapeDtypeStruct(value.shape, value.dtype),
        in_specs=[anywhere, anywhere],
        out_specs=anywhere,
        input_output_aliases={0: 0},
    )(value, tie)


def halve(value, axis, dim, left, bit):
    at = dim + left.index(bit)
    mine = bit_of(axis, bit)
    keep = lax.dynamic_index_in_dim(value, mine, at, keepdims=False)
    give = lax.dynamic_index_in_dim(value, 1 - mine, at, keepdims=False)
    total = keep.astype(F32) + partner_2(give, axis, bit).astype(F32)
    return total, [other for other in left if other != bit], give


def halved_sum(value, axis, dim, order, ties=()):
    left = list(reversed(range(bits_of(axis))))
    shape = value.shape
    value = value.reshape(shape[:dim] + (2,) * len(left) + shape[dim + 1 :])
    sent = []
    firsts = None
    for step, bit in enumerate(order):
        if step < len(ties) and ties[step] is not None:
            value = hold(value, ties[step])
        total, left, give = halve(value, axis, dim, left, bit)
        value = total.astype(BF)
        firsts = value if step == 0 else firsts
        sent.append(give)
    return total, (sent[0], firsts)


def doubled_gather(value, axis):
    shape = value.shape
    count = 0
    for bit in reversed(range(bits_of(axis))):
        other = partner_2(value, axis, bit)
        low = bit_of(axis, bit) == 0
        value = jnp.stack(
            [jnp.where(low, value, other), jnp.where(low, other, value)], axis=count
        )
        count += 1
    return value.reshape((lax.axis_size(axis),) + shape)


def exchanged_sum(value, axis):
    kind = value.dtype
    for bit in range(bits_of(axis)):
        total = value.astype(F32) + partner_2(value, axis, bit).astype(F32)
        value = total.astype(kind)
    return total


def lanes(index, width):
    return pl.ds(pl.multiple_of(index * width, width), width)


def pair_of(index, level):
    low = 2**level
    first = (index // low) * (2 * low) + index % low
    return first, first + low


def pair_matrix(w_self, w_cross, first, second):
    top = jnp.concatenate([w_self[0, first], w_cross[0, second]], axis=1)
    bottom = jnp.concatenate([w_cross[0, first], w_self[0, second]], axis=1)
    return jnp.concatenate([top, bottom], axis=0)


def side_by_side(ref, first, second, width):
    return jnp.concatenate([ref[:, lanes(first, width)], ref[:, lanes(second, width)]], axis=1)


def blocks_of(ref, first, second, width):
    per = ref.shape[2] // width
    return jnp.concatenate(
        [ref[i // per, :, lanes(lax.rem(i, per), width)] for i in (first, second)], axis=1
    )


def put_chunks(out, total):
    count, _, size = out.shape
    for chunk in range(count):
        out[chunk] = total[:, chunk * size : (chunk + 1) * size].astype(BF)


def up_kernel(levels, slots, width, pairs, hidden, w_up, *refs):
    w_self, w_cross, states = refs[:levels], refs[levels : 2 * levels], refs[2 * levels :]

    @pl.loop(0, slots, unroll=UNROLL)
    def _(j):
        both = blocks_of(hidden, pairs[j, 0], pairs[j, 1], width)
        matrix = jnp.concatenate([w_up[j, 0], w_up[j, 1]], axis=0)
        states[0][:, lanes(j, width)] = dot_nn(both, matrix).astype(BF)

    for level in range(levels):

        @pl.loop(0, slots // 2, unroll=UNROLL)
        def _(index):
            first, second = pair_of(index, level)
            both = side_by_side(states[level], first, second, width)
            result = dot_nn(both, pair_matrix(w_self[level], w_cross[level], first, second)).astype(BF)
            states[level + 1][:, lanes(first, width)] = result[:, :width]
            states[level + 1][:, lanes(second, width)] = result[:, width:]


def across_kernel(slots, width, state, partner, w_self, w_cross, out):
    @pl.loop(0, slots, unroll=UNROLL)
    def _(j):
        both = jnp.concatenate([state[:, lanes(j, width)], partner[:, lanes(j, width)]], axis=1)
        matrix = jnp.concatenate([w_self[0, j], w_cross[0, j]], axis=0)
        out[:, lanes(j, width)] = dot_nn(both, matrix).astype(BF)


def top_kernel(
    slots, width, pairs, state, partner, w_self, w_cross, w_down, cotangent, down, grad, send, total
):
    total[...] = jnp.zeros_like(total)

    @pl.loop(0, slots, unroll=UNROLL)
    def _(j):
        first, second = pairs[j, 0], pairs[j, 1]
        both = jnp.concatenate([state[:, lanes(j, width)], partner[:, lanes(j, width)]], axis=1)
        matrix = jnp.concatenate([w_self[0, j], w_cross[0, j]], axis=0)
        top = dot_nn(both, matrix).astype(BF).astype(F32)
        root = math.sqrt(2.0 / math.pi)
        square = top * top
        bend = jnp.tanh(root * (top + 0.044715 * (square * top)))
        active = (0.5 * top * (1.0 + bend)).astype(BF)
        slope = 0.5 * (1.0 + bend) + 0.5 * top * (1.0 - bend * bend) * (
            root * (1.0 + (3 * 0.044715) * square)
        )
        w_both = jnp.concatenate([w_down[j, 0], w_down[j, 1]], axis=1)
        pieces = dot_nn(active, w_both)
        total[:, lanes(first, width)] += pieces[:, :width]
        total[:, lanes(second, width)] += pieces[:, width:]
        grad_act = dot_nt(blocks_of(cotangent, first, second, width), w_both)
        grad_top = (grad_act * slope).astype(BF)
        grad[:, lanes(j, width)] = grad_top
        send[:, lanes(j, width)] = dot_nt(grad_top, w_cross[0, j]).astype(BF)

    put_chunks(down, total)


def across_grad_kernel(slots, width, state, partner, grad, after, terms):
    @pl.loop(0, slots, unroll=UNROLL)
    def _(j):
        both = jnp.concatenate([state[:, lanes(j, width)], partner[:, lanes(j, width)]], axis=1)
        result = dot_tn(both, grad[:, lanes(j, width)]).astype(BF)
        terms[0, 0, j] = result[:width]
        terms[0, 1, j] = result[width:]


def middle_kernel(slots, width, grad, incoming, w_self, w_cross_below, after, out, send):
    @pl.loop(0, slots, unroll=UNROLL)
    def _(j):
        own = dot_nt(grad[:, lanes(j, width)], w_self[0, j])
        result = (own + incoming[:, lanes(j, width)].astype(F32)).astype(BF)
        out[:, lanes(j, width)] = result
        send[:, lanes(j, width)] = dot_nt(result, w_cross_below[0, j]).astype(BF)


def down_kernel(levels, slots, width, pairs, grad, incoming, w_self_above, w_up, *refs):
    w_self, w_cross = refs[:levels], refs[levels : 2 * levels]
    grads = refs[2 * levels : 3 * levels + 1]
    spread, total = refs[3 * levels + 1 :]

    @pl.loop(0, slots, unroll=UNROLL)
    def _(j):
        own = dot_nt(grad[:, lanes(j, width)], w_self_above[0, j])
        result = own + incoming[:, lanes(j, width)].astype(F32)
        grads[levels][:, lanes(j, width)] = result.astype(BF)

    for level in reversed(range(levels)):

        @pl.loop(0, slots // 2, unroll=UNROLL)
        def _(index):
            first, second = pair_of(index, level)
            both = side_by_side(grads[level + 1], first, second, width)
            result = dot_nt(both, pair_matrix(w_self[level], w_cross[level], first, second)).astype(BF)
            grads[level][:, lanes(first, width)] = result[:, :width]
            grads[level][:, lanes(second, width)] = result[:, width:]

    total[...] = jnp.zeros_like(total)

    @pl.loop(0, slots, unroll=UNROLL)
    def _(j):
        matrix = jnp.concatenate([w_up[j, 0], w_up[j, 1]], axis=0)
        pieces = dot_nt(grads[0][:, lanes(j, width)], matrix)
        total[:, lanes(pairs[j, 0], width)] += pieces[:, :width]
        total[:, lanes(pairs[j, 1], width)] += pieces[:, width:]

    put_chunks(spread, total)


def pair_grad_kernel(group, slots, width, *refs):
    count = len(group)
    states, grads, terms = refs[:count], refs[count : 2 * count], refs[2 * count + 1]
    for at, level in enumerate(group):

        @pl.loop(0, slots // 2, unroll=UNROLL)
        def _(index):
            first, second = pair_of(index, level)
            result = dot_tn(
                side_by_side(states[at], first, second, width),
                side_by_side(grads[at], first, second, width),
            ).astype(BF)
            terms[at, 0, first] = result[:width, :width]
            terms[at, 1, second] = result[:width, width:]
            terms[at, 1, first] = result[width:, :width]
            terms[at, 0, second] = result[width:, width:]


def whole(array):
    return pl.BlockSpec(array.shape, lambda i: (0,) * array.ndim)


def level_of(array, level):
    return pl.BlockSpec((1,) + array.shape[1:], lambda i: (level, 0, 0, 0))


def rows_of(shape, tile):
    return pl.BlockSpec((tile, shape[1]), lambda i: (i, 0))


def chunk_rows_of(shape, tile):
    return pl.BlockSpec((shape[0], tile, shape[2]), lambda i: (0, i, 0))


def call(kernel, steps, operands, in_specs, out_shapes, out_specs, flops, scratch=()):
    moved = sum(x.size * x.dtype.itemsize for x in operands[:4])
    moved += sum(math.prod(x.shape) * x.dtype.itemsize for x in out_shapes)
    return pl.pallas_call(
        kernel,
        grid=(steps,),
        in_specs=in_specs,
        out_specs=out_specs,
        out_shape=out_shapes,
        scratch_shapes=scratch,
        compiler_params=pltpu.CompilerParams(vmem_limit_bytes=VMEM_BYTES),
        cost_estimate=pl.CostEstimate(flops=flops, bytes_accessed=moved, transcendentals=0),
    )(*operands)


def per_device(
    tokens, w_first, second_factor_weight, w_up, w_self, w_cross, w_down, block_pairs, cotangent
):
    seq_len, width_local = tokens.shape
    levels, slots, width, _ = w_self.shape
    model_width = width_local * lax.axis_size("tp")
    local = slots.bit_length() - 1
    hidden_width = slots * width
    total_tokens = seq_len * lax.axis_size("seq")
    token_scale = 1.0 / math.sqrt(total_tokens)
    model_width_scale = 1.0 / math.sqrt(model_width)
    positions, groups, _ = second_factor_weight.shape
    tile = seq_len // 2
    steps = 2
    smem = pl.BlockSpec(memory_space=pltpu.SMEM)
    state_shape = jax.ShapeDtypeStruct((seq_len, hidden_width), BF)
    model_shape = jax.ShapeDtypeStruct((lax.axis_size("tp"), seq_len, width_local), BF)
    seq_size = lax.axis_size("seq")

    def terms_of(count):
        return jax.ShapeDtypeStruct((count, 2, slots, width, width), BF)

    seq_bits = list(range(bits_of("seq")))
    orders = [seq_bits, seq_bits[1:2] + seq_bits[:1] + seq_bits[2:]]
    tp_bits = list(range(bits_of("tp")))

    def summed(result, order, ties=()):
        chunked = result.reshape(result.shape[:3] + (seq_size, width // seq_size, width))
        return halved_sum(chunked, "seq", 3, order, ties)[0]

    row_state = rows_of(state_shape.shape, tile)
    row_model = chunk_rows_of(model_shape.shape, tile)
    unit = 2 * seq_len * hidden_width * width

    cotangent_all = doubled_gather(cotangent, "tp")

    same = jnp.eye(positions, dtype=BF)
    mixer = (
        second_factor_weight.transpose(1, 0, 2)[:, :, :, None] * same[None, :, None, :]
    ).reshape(groups * positions, groups * positions)

    first_factor = w_first[0]
    first_out = dot_nn(first_factor, tokens).astype(BF)
    first_rows = lax.all_to_all(first_out, "seq", split_axis=0, concat_axis=0, tiled=True)
    mixed_part = dot_nn(mixer, first_rows).astype(BF)
    mixed = lax.all_to_all(mixed_part, "seq", split_axis=0, concat_axis=0, tiled=True)
    hidden_in = (tokens.astype(F32) + mixed.astype(F32)).astype(BF)
    hidden_all = doubled_gather(hidden_in, "tp")

    local_self = [w_self] * local
    local_cross = [w_cross] * local
    local_specs = [level_of(w_self, level) for level in range(local)]
    states = call(
        functools.partial(up_kernel, local, slots, width),
        steps,
        [block_pairs, hidden_all, w_up, *local_self, *local_cross],
        [smem, row_model, whole(w_up), *local_specs, *local_specs],
        [state_shape] * (local + 1),
        [row_state] * (local + 1),
        (local + 1) * 2 * unit,
    )
    states = list(states)
    partners = [None] * levels
    for level in range(local, levels - 1):
        partners[level] = partner_2(states[level], "tp", level - local)
        (state,) = call(
            functools.partial(across_kernel, slots, width),
            steps,
            [states[level], partners[level], w_self, w_cross],
            [row_state, row_state, level_of(w_self, level), level_of(w_cross, level)],
            [state_shape],
            [row_state],
            2 * unit,
        )
        states.append(state)
    last = levels - 1
    partners[last] = partner_2(states[last], "tp", last - local)
    down_part, grad, send = call(
        functools.partial(top_kernel, slots, width),
        steps,
        [block_pairs, states[last], partners[last], w_self, w_cross, w_down, cotangent_all],
        [
            smem,
            row_state,
            row_state,
            level_of(w_self, last),
            level_of(w_cross, last),
            whole(w_down),
            row_model,
        ],
        [model_shape, state_shape, state_shape],
        [row_model, row_state, row_state],
        7 * unit,
        [pltpu.VMEM((tile, model_width), F32)],
    )
    terms = [None] * levels

    anywhere = pl.BlockSpec(memory_space=pl.ANY)

    def across_terms(level, gradient, after):
        (result,) = call(
            functools.partial(across_grad_kernel, slots, width),
            1,
            [states[level], partners[level], gradient, after],
            [whole(states[level]), whole(states[level]), whole(gradient), anywhere],
            [terms_of(1)],
            [whole(terms_of(1))],
            2 * unit,
        )
        return result

    for level in range(last, local, -1):
        incoming = partner_2(send, "tp", level - local)
        result = across_terms(level, grad, send)
        terms[level] = summed(result, orders[level % 2])[0]
        grad, send = call(
            functools.partial(middle_kernel, slots, width),
            steps,
            [grad, incoming, w_self, w_cross, result],
            [
                row_state,
                row_state,
                level_of(w_self, level),
                level_of(w_cross, level - 1),
                anywhere,
            ],
            [state_shape, state_shape],
            [row_state, row_state],
            2 * unit,
        )
    incoming = partner_2(send, "tp", 0)
    grad_above = grad
    *grads, spread = call(
        functools.partial(down_kernel, local, slots, width),
        steps,
        [block_pairs, grad, incoming, w_self, w_up, *local_self, *local_cross],
        [
            smem,
            row_state,
            row_state,
            level_of(w_self, local),
            whole(w_up),
            *local_specs,
            *local_specs,
        ],
        [state_shape] * (local + 1) + [model_shape],
        [row_state] * (local + 1) + [row_model],
        (2 * local + 3) * unit,
        [pltpu.VMEM((tile, model_width), F32)],
    )
    spread_part, (spread_sent, spread_first) = halved_sum(spread, "tp", 0, tp_bits)
    grad_hidden = (cotangent.astype(F32) + spread_part).astype(BF)
    down_sum, _ = halved_sum(down_part, "tp", 0, tp_bits)
    layer_out = (hidden_in.astype(F32) + down_sum).astype(BF)

    grad_rows = lax.all_to_all(grad_hidden, "seq", split_axis=0, concat_axis=0, tiled=True)
    moved_back = dot_tn(mixer, grad_rows).astype(BF)
    returned = lax.all_to_all(moved_back, "seq", split_axis=0, concat_axis=0, tiled=True)
    ties = [None, grad_rows, returned]
    result = across_terms(local, grad_above, spread_sent)
    terms[local] = summed(result, orders[local % 2], ties)[0]
    for top in range(local, 0, -2):
        group = list(range(max(top - 2, 0), top))
        (result,) = call(
            functools.partial(pair_grad_kernel, group, slots, width),
            1,
            [states[level] for level in group]
            + [grads[level + 1] for level in group]
            + [spread_first],
            [whole(states[0])] * (2 * len(group)) + [anywhere],
            [terms_of(len(group))],
            [whole(terms_of(len(group)))],
            2 * len(group) * unit,
        )
        sums = summed(result, orders[(local - top) // 2 % 2], ties)
        for at, level in enumerate(group):
            terms[level] = sums[at]

    cross_rows = dot_nt(grad_rows, first_rows).reshape(groups, positions, groups, positions)
    second_part = jnp.sum(cross_rows * same.astype(F32)[None, :, None, :], axis=3).transpose(1, 0, 2)
    first_part = dot_nt(returned, tokens).astype(BF)
    second_sum = exchanged_sum(second_part, "tp")
    first_sum = exchanged_sum(first_part, "tp")
    grad_mix = dot_tn(first_factor, returned)
    grad_tokens = (grad_hidden.astype(F32) + grad_mix).astype(BF)
    level_terms = jnp.stack(terms, axis=1) * token_scale
    return (
        layer_out,
        grad_tokens,
        (first_sum * model_width_scale)[None],
        second_sum * model_width_scale,
        level_terms[0],
        level_terms[1],
    )


def solution(mesh):
    in_specs = (
        P("seq", "tp"),
        P("seq", None, None),
        P("seq", None, None),
        P("tp", None, None, None),
        P(None, "tp", None, None),
        P(None, "tp", None, None),
        P("tp", None, None, None),
        P("tp", None),
        P("seq", "tp"),
    )
    out_specs = (
        P("seq", "tp"),
        P("seq", "tp"),
        P("seq", None, None),
        P("seq", None, None),
        P(None, "tp", "seq", None),
        P(None, "tp", "seq", None),
    )
    return jax.shard_map(
        per_device, mesh=mesh, in_specs=in_specs, out_specs=out_specs, check_vma=False
    )
```

```python
import functools
import math

import jax
import jax.numpy as jnp
from jax import lax
from jax.experimental import pallas as pl
from jax.experimental.pallas import tpu as pltpu
from jax.sharding import PartitionSpec as P

BF = jnp.bfloat16
F32 = jnp.float32
VMEM_BYTES = 56 * 1024 * 1024
UNROLL = 4


def dot(left, right, contract):
    return lax.dot_general(left, right, (contract, ((), ())), preferred_element_type=F32)


def dot_nn(left, right):
    return dot(left, right, ((1,), (0,)))


def dot_nt(left, right):
    return dot(left, right, ((1,), (1,)))


def dot_tn(left, right):
    return dot(left, right, ((0,), (0,)))


def partner_2(value, axis, bit):
    mask = 2**bit
    pairs = [(source, source ^ mask) for source in range(lax.axis_size(axis))]
    return lax.ppermute(value, axis, pairs)


def bit_of(axis, bit):
    return (lax.axis_index(axis) // 2**bit) % 2


def bits_of(axis):
    return lax.axis_size(axis).bit_length() - 1


def nothing(value, tie, out):
    pass


def hold(value, tie):
    anywhere = pl.BlockSpec(memory_space=pl.ANY)
    return pl.pallas_call(
        nothing,
        out_shape=jax.ShapeDtypeStruct(value.shape, value.dtype),
        in_specs=[anywhere, anywhere],
        out_specs=anywhere,
        input_output_aliases={0: 0},
    )(value, tie)


def halve(value, axis, dim, left, bit):
    at = dim + left.index(bit)
    mine = bit_of(axis, bit)
    keep = lax.dynamic_index_in_dim(value, mine, at, keepdims=False)
    give = lax.dynamic_index_in_dim(value, 1 - mine, at, keepdims=False)
    total = keep.astype(F32) + partner_2(give, axis, bit).astype(F32)
    return total, [other for other in left if other != bit], give


def halved_sum(value, axis, dim, order, ties=()):
    left = list(reversed(range(bits_of(axis))))
    shape = value.shape
    value = value.reshape(shape[:dim] + (2,) * len(left) + shape[dim + 1 :])
    sent = []
    firsts = None
    for step, bit in enumerate(order):
        if step < len(ties) and ties[step] is not None:
            value = hold(value, ties[step])
        total, left, give = halve(value, axis, dim, left, bit)
        value = total.astype(BF)
        firsts = value if step == 0 else firsts
        sent.append(give)
    return total, (sent[0], firsts)


def doubled_gather(value, axis):
    shape = value.shape
    count = 0
    for bit in reversed(range(bits_of(axis))):
        other = partner_2(value, axis, bit)
        low = bit_of(axis, bit) == 0
        value = jnp.stack(
            [jnp.where(low, value, other), jnp.where(low, other, value)], axis=count
        )
        count += 1
    return value.reshape((lax.axis_size(axis),) + shape)


def exchanged_sum(value, axis):
    kind = value.dtype
    for bit in range(bits_of(axis)):
        total = value.astype(F32) + partner_2(value, axis, bit).astype(F32)
        value = total.astype(kind)
        if bit == 0:
            first = value
    return total, first


def lanes(index, width):
    return pl.ds(pl.multiple_of(index * width, width), width)


def pair_of(index, level):
    low = 2**level
    first = (index // low) * (2 * low) + index % low
    return first, first + low


def pair_matrix(w_self, w_cross, first, second):
    top = jnp.concatenate([w_self[0, first], w_cross[0, second]], axis=1)
    bottom = jnp.concatenate([w_cross[0, first], w_self[0, second]], axis=1)
    return jnp.concatenate([top, bottom], axis=0)


def side_by_side(ref, first, second, width):
    return jnp.concatenate([ref[:, lanes(first, width)], ref[:, lanes(second, width)]], axis=1)


def blocks_of(ref, first, second, width):
    per = ref.shape[2] // width
    return jnp.concatenate(
        [ref[i // per, :, lanes(lax.rem(i, per), width)] for i in (first, second)], axis=1
    )


def put_chunks(out, total):
    count, _, size = out.shape
    for chunk in range(count):
        out[chunk] = total[:, chunk * size : (chunk + 1) * size].astype(BF)


def up_kernel(levels, slots, width, pairs, hidden, w_up, *refs):
    w_self, w_cross, states = refs[:levels], refs[levels : 2 * levels], refs[2 * levels :]

    @pl.loop(0, slots, unroll=UNROLL)
    def _(j):
        both = blocks_of(hidden, pairs[j, 0], pairs[j, 1], width)
        matrix = jnp.concatenate([w_up[j, 0], w_up[j, 1]], axis=0)
        states[0][:, lanes(j, width)] = dot_nn(both, matrix).astype(BF)

    for level in range(levels):

        @pl.loop(0, slots // 2, unroll=UNROLL)
        def _(index):
            first, second = pair_of(index, level)
            both = side_by_side(states[level], first, second, width)
            result = dot_nn(both, pair_matrix(w_self[level], w_cross[level], first, second)).astype(BF)
            states[level + 1][:, lanes(first, width)] = result[:, :width]
            states[level + 1][:, lanes(second, width)] = result[:, width:]


def across_kernel(slots, width, state, partner, w_self, w_cross, out):
    @pl.loop(0, slots, unroll=UNROLL)
    def _(j):
        both = jnp.concatenate([state[:, lanes(j, width)], partner[:, lanes(j, width)]], axis=1)
        matrix = jnp.concatenate([w_self[0, j], w_cross[0, j]], axis=0)
        out[:, lanes(j, width)] = dot_nn(both, matrix).astype(BF)


def top_kernel(
    slots, width, pairs, state, partner, w_self, w_cross, w_down, cotangent, down, grad, send, total
):
    total[...] = jnp.zeros_like(total)

    @pl.loop(0, slots, unroll=UNROLL)
    def _(j):
        first, second = pairs[j, 0], pairs[j, 1]
        both = jnp.concatenate([state[:, lanes(j, width)], partner[:, lanes(j, width)]], axis=1)
        matrix = jnp.concatenate([w_self[0, j], w_cross[0, j]], axis=0)
        top = dot_nn(both, matrix).astype(BF).astype(F32)
        root = math.sqrt(2.0 / math.pi)
        square = top * top
        bend = jnp.tanh(root * (top + 0.044715 * (square * top)))
        active = (0.5 * top * (1.0 + bend)).astype(BF)
        slope = 0.5 * (1.0 + bend) + 0.5 * top * (1.0 - bend * bend) * (
            root * (1.0 + (3 * 0.044715) * square)
        )
        w_both = jnp.concatenate([w_down[j, 0], w_down[j, 1]], axis=1)
        pieces = dot_nn(active, w_both)
        total[:, lanes(first, width)] += pieces[:, :width]
        total[:, lanes(second, width)] += pieces[:, width:]
        grad_act = dot_nt(blocks_of(cotangent, first, second, width), w_both)
        grad_top = (grad_act * slope).astype(BF)
        grad[:, lanes(j, width)] = grad_top
        send[:, lanes(j, width)] = dot_nt(grad_top, w_cross[0, j]).astype(BF)

    put_chunks(down, total)


def across_grad_kernel(slots, width, state, partner, grad, after, terms):
    @pl.loop(0, slots, unroll=UNROLL)
    def _(j):
        both = jnp.concatenate([state[:, lanes(j, width)], partner[:, lanes(j, width)]], axis=1)
        result = dot_tn(both, grad[:, lanes(j, width)]).astype(BF)
        terms[0, 0, j] = result[:width]
        terms[0, 1, j] = result[width:]


def middle_kernel(slots, width, grad, incoming, w_self, w_cross_below, after, out, send):
    @pl.loop(0, slots, unroll=UNROLL)
    def _(j):
        own = dot_nt(grad[:, lanes(j, width)], w_self[0, j])
        result = (own + incoming[:, lanes(j, width)].astype(F32)).astype(BF)
        out[:, lanes(j, width)] = result
        send[:, lanes(j, width)] = dot_nt(result, w_cross_below[0, j]).astype(BF)


def down_kernel(levels, slots, width, pairs, grad, incoming, w_self_above, w_up, *refs):
    w_self, w_cross = refs[:levels], refs[levels : 2 * levels]
    grads = refs[2 * levels : 3 * levels + 1]
    spread, total = refs[3 * levels + 1 :]

    @pl.loop(0, slots, unroll=UNROLL)
    def _(j):
        own = dot_nt(grad[:, lanes(j, width)], w_self_above[0, j])
        result = own + incoming[:, lanes(j, width)].astype(F32)
        grads[levels][:, lanes(j, width)] = result.astype(BF)

    for level in reversed(range(levels)):

        @pl.loop(0, slots // 2, unroll=UNROLL)
        def _(index):
            first, second = pair_of(index, level)
            both = side_by_side(grads[level + 1], first, second, width)
            result = dot_nt(both, pair_matrix(w_self[level], w_cross[level], first, second)).astype(BF)
            grads[level][:, lanes(first, width)] = result[:, :width]
            grads[level][:, lanes(second, width)] = result[:, width:]

    total[...] = jnp.zeros_like(total)

    @pl.loop(0, slots, unroll=UNROLL)
    def _(j):
        matrix = jnp.concatenate([w_up[j, 0], w_up[j, 1]], axis=0)
        pieces = dot_nt(grads[0][:, lanes(j, width)], matrix)
        total[:, lanes(pairs[j, 0], width)] += pieces[:, :width]
        total[:, lanes(pairs[j, 1], width)] += pieces[:, width:]

    put_chunks(spread, total)


def pair_grad_kernel(group, slots, width, *refs):
    count = len(group)
    states, grads, terms = refs[:count], refs[count : 2 * count], refs[2 * count + 1]
    for at, level in enumerate(group):

        @pl.loop(0, slots // 2, unroll=UNROLL)
        def _(index):
            first, second = pair_of(index, level)
            result = dot_tn(
                side_by_side(states[at], first, second, width),
                side_by_side(grads[at], first, second, width),
            ).astype(BF)
            terms[at, 0, first] = result[:width, :width]
            terms[at, 1, second] = result[:width, width:]
            terms[at, 1, first] = result[width:, :width]
            terms[at, 0, second] = result[width:, width:]


def whole(array):
    return pl.BlockSpec(array.shape, lambda i: (0,) * array.ndim)


def level_of(array, level):
    return pl.BlockSpec((1,) + array.shape[1:], lambda i: (level, 0, 0, 0))


def rows_of(shape, tile):
    return pl.BlockSpec((tile, shape[1]), lambda i: (i, 0))


def chunk_rows_of(shape, tile):
    return pl.BlockSpec((shape[0], tile, shape[2]), lambda i: (0, i, 0))


def call(kernel, steps, operands, in_specs, out_shapes, out_specs, flops, scratch=()):
    moved = sum(x.size * x.dtype.itemsize for x in operands[:4])
    moved += sum(math.prod(x.shape) * x.dtype.itemsize for x in out_shapes)
    return pl.pallas_call(
        kernel,
        grid=(steps,),
        in_specs=in_specs,
        out_specs=out_specs,
        out_shape=out_shapes,
        scratch_shapes=scratch,
        compiler_params=pltpu.CompilerParams(vmem_limit_bytes=VMEM_BYTES),
        cost_estimate=pl.CostEstimate(flops=flops, bytes_accessed=moved, transcendentals=0),
    )(*operands)


def per_device(
    tokens, w_first, second_factor_weight, w_up, w_self, w_cross, w_down, block_pairs, cotangent
):
    seq_len, width_local = tokens.shape
    levels, slots, width, _ = w_self.shape
    model_width = width_local * lax.axis_size("tp")
    local = slots.bit_length() - 1
    hidden_width = slots * width
    total_tokens = seq_len * lax.axis_size("seq")
    token_scale = 1.0 / math.sqrt(total_tokens)
    model_width_scale = 1.0 / math.sqrt(model_width)
    positions, groups, _ = second_factor_weight.shape
    tile = seq_len // 2
    steps = 2
    smem = pl.BlockSpec(memory_space=pltpu.SMEM)
    state_shape = jax.ShapeDtypeStruct((seq_len, hidden_width), BF)
    model_shape = jax.ShapeDtypeStruct((lax.axis_size("tp"), seq_len, width_local), BF)
    seq_size = lax.axis_size("seq")

    def terms_of(count):
        return jax.ShapeDtypeStruct((count, 2, slots, width, width), BF)

    seq_bits = list(range(bits_of("seq")))
    orders = [seq_bits, seq_bits[1:2] + seq_bits[:1] + seq_bits[2:]]
    tp_bits = list(range(bits_of("tp")))

    def chunks_of(result):
        return result.reshape(result.shape[:3] + (seq_size, width // seq_size, width))

    def first_given(result, order):
        left = list(reversed(range(bits_of("seq"))))
        chunked = chunks_of(result)
        chunked = chunked.reshape(chunked.shape[:3] + (2,) * len(left) + chunked.shape[4:])
        return halve(chunked, "seq", 3, left, order[0])[2]

    def summed(result, order, ties=()):
        chunked = chunks_of(result)
        return halved_sum(chunked, "seq", 3, order, ties)[0]

    row_state = rows_of(state_shape.shape, tile)
    row_model = chunk_rows_of(model_shape.shape, tile)
    unit = 2 * seq_len * hidden_width * width

    cotangent_all = doubled_gather(cotangent, "tp")

    same = jnp.eye(positions, dtype=BF)
    mixer = (
        second_factor_weight.transpose(1, 0, 2)[:, :, :, None] * same[None, :, None, :]
    ).reshape(groups * positions, groups * positions)

    first_factor = w_first[0]
    first_out = dot_nn(first_factor, tokens).astype(BF)
    first_rows = lax.all_to_all(first_out, "seq", split_axis=0, concat_axis=0, tiled=True)
    mixed_part = dot_nn(mixer, first_rows).astype(BF)
    mixed = lax.all_to_all(mixed_part, "seq", split_axis=0, concat_axis=0, tiled=True)
    hidden_in = (tokens.astype(F32) + mixed.astype(F32)).astype(BF)
    hidden_all = doubled_gather(hidden_in, "tp")

    local_self = [w_self] * local
    local_cross = [w_cross] * local
    local_specs = [level_of(w_self, level) for level in range(local)]
    states = call(
        functools.partial(up_kernel, local, slots, width),
        steps,
        [block_pairs, hidden_all, w_up, *local_self, *local_cross],
        [smem, row_model, whole(w_up), *local_specs, *local_specs],
        [state_shape] * (local + 1),
        [row_state] * (local + 1),
        (local + 1) * 2 * unit,
    )
    states = list(states)
    partners = [None] * levels
    for level in range(local, levels - 1):
        partners[level] = partner_2(states[level], "tp", level - local)
        (state,) = call(
            functools.partial(across_kernel, slots, width),
            steps,
            [states[level], partners[level], w_self, w_cross],
            [row_state, row_state, level_of(w_self, level), level_of(w_cross, level)],
            [state_shape],
            [row_state],
            2 * unit,
        )
        states.append(state)
    last = levels - 1
    partners[last] = partner_2(states[last], "tp", last - local)
    down_part, grad, send = call(
        functools.partial(top_kernel, slots, width),
        steps,
        [block_pairs, states[last], partners[last], w_self, w_cross, w_down, cotangent_all],
        [
            smem,
            row_state,
            row_state,
            level_of(w_self, last),
            level_of(w_cross, last),
            whole(w_down),
            row_model,
        ],
        [model_shape, state_shape, state_shape],
        [row_model, row_state, row_state],
        7 * unit,
        [pltpu.VMEM((tile, model_width), F32)],
    )
    terms = [None] * levels

    anywhere = pl.BlockSpec(memory_space=pl.ANY)

    def across_terms(level, gradient, after):
        (result,) = call(
            functools.partial(across_grad_kernel, slots, width),
            1,
            [states[level], partners[level], gradient, after],
            [whole(states[level]), whole(states[level]), whole(gradient), anywhere],
            [terms_of(1)],
            [whole(terms_of(1))],
            2 * unit,
        )
        return result

    early = []
    for level in range(last, local, -1):
        incoming = partner_2(send, "tp", level - local)
        result = across_terms(level, grad, send)
        early.append((level, result))
        given = first_given(result, orders[level % 2])
        grad, send = call(
            functools.partial(middle_kernel, slots, width),
            steps,
            [grad, incoming, w_self, w_cross, given],
            [
                row_state,
                row_state,
                level_of(w_self, level),
                level_of(w_cross, level - 1),
                anywhere,
            ],
            [state_shape, state_shape],
            [row_state, row_state],
            2 * unit,
        )
    incoming = partner_2(send, "tp", 0)
    grad_above = grad
    *grads, spread = call(
        functools.partial(down_kernel, local, slots, width),
        steps,
        [block_pairs, grad, incoming, w_self, w_up, *local_self, *local_cross],
        [
            smem,
            row_state,
            row_state,
            level_of(w_self, local),
            whole(w_up),
            *local_specs,
            *local_specs,
        ],
        [state_shape] * (local + 1) + [model_shape],
        [row_state] * (local + 1) + [row_model],
        (2 * local + 3) * unit,
        [pltpu.VMEM((tile, model_width), F32)],
    )
    spread_part, (spread_sent, spread_first) = halved_sum(spread, "tp", 0, tp_bits)
    grad_hidden = (cotangent.astype(F32) + spread_part).astype(BF)
    down_sum, _ = halved_sum(down_part, "tp", 0, tp_bits)
    layer_out = (hidden_in.astype(F32) + down_sum).astype(BF)

    grad_rows = lax.all_to_all(grad_hidden, "seq", split_axis=0, concat_axis=0, tiled=True)
    moved_back = dot_tn(mixer, grad_rows).astype(BF)
    returned = lax.all_to_all(moved_back, "seq", split_axis=0, concat_axis=0, tiled=True)
    first_part = dot_nt(returned, tokens).astype(BF)
    first_sum, first_hop = exchanged_sum(first_part, "tp")
    ties = [None, grad_rows, first_hop]
    for level, result in early:
        terms[level] = summed(result, orders[level % 2], [None, spread, grad_rows])[0]
    result = across_terms(local, grad_above, spread_sent)
    terms[local] = summed(result, orders[local % 2], ties)[0]
    for top in range(local, 0, -2):
        group = list(range(max(top - 2, 0), top))
        (result,) = call(
            functools.partial(pair_grad_kernel, group, slots, width),
            1,
            [states[level] for level in group]
            + [grads[level + 1] for level in group]
            + [spread_first],
            [whole(states[0])] * (2 * len(group)) + [anywhere],
            [terms_of(len(group))],
            [whole(terms_of(len(group)))],
            2 * len(group) * unit,
        )
        sums = summed(result, orders[(local - top) // 2 % 2], ties)
        for at, level in enumerate(group):
            terms[level] = sums[at]

    cross_rows = dot_nt(grad_rows, first_rows).reshape(groups, positions, groups, positions)
    second_part = jnp.sum(cross_rows * same.astype(F32)[None, :, None, :], axis=3).transpose(1, 0, 2)
    second_sum, _ = exchanged_sum(second_part, "tp")
    grad_mix = dot_tn(first_factor, returned)
    grad_tokens = (grad_hidden.astype(F32) + grad_mix).astype(BF)
    level_terms = jnp.stack(terms, axis=1) * token_scale
    return (
        layer_out,
        grad_tokens,
        (first_sum * model_width_scale)[None],
        second_sum * model_width_scale,
        level_terms[0],
        level_terms[1],
    )


def solution(mesh):
    in_specs = (
        P("seq", "tp"),
        P("seq", None, None),
        P("seq", None, None),
        P("tp", None, None, None),
        P(None, "tp", None, None),
        P(None, "tp", None, None),
        P("tp", None, None, None),
        P("tp", None),
        P("seq", "tp"),
    )
    out_specs = (
        P("seq", "tp"),
        P("seq", "tp"),
        P("seq", None, None),
        P("seq", None, None),
        P(None, "tp", "seq", None),
        P(None, "tp", "seq", None),
    )
    return jax.shard_map(
        per_device, mesh=mesh, in_specs=in_specs, out_specs=out_specs, check_vma=False
    )
```

```python
import functools
import math

import jax
import jax.numpy as jnp
from jax import lax
from jax.experimental import pallas as pl
from jax.experimental.pallas import tpu as pltpu
from jax.sharding import PartitionSpec as P

BF = jnp.bfloat16
F32 = jnp.float32
VMEM_BYTES = 56 * 1024 * 1024
UNROLL = 4


def dot(left, right, contract):
    return lax.dot_general(left, right, (contract, ((), ())), preferred_element_type=F32)


def dot_nn(left, right):
    return dot(left, right, ((1,), (0,)))


def dot_nt(left, right):
    return dot(left, right, ((1,), (1,)))


def dot_tn(left, right):
    return dot(left, right, ((0,), (0,)))


def partner_2(value, axis, bit):
    mask = 2**bit
    pairs = [(source, source ^ mask) for source in range(lax.axis_size(axis))]
    return lax.ppermute(value, axis, pairs)


def bit_of(axis, bit):
    return (lax.axis_index(axis) // 2**bit) % 2


def bits_of(axis):
    return lax.axis_size(axis).bit_length() - 1


def nothing(value, tie, out):
    pass


def hold(value, tie):
    anywhere = pl.BlockSpec(memory_space=pl.ANY)
    return pl.pallas_call(
        nothing,
        out_shape=jax.ShapeDtypeStruct(value.shape, value.dtype),
        in_specs=[anywhere, anywhere],
        out_specs=anywhere,
        input_output_aliases={0: 0},
    )(value, tie)


def halve(value, axis, dim, left, bit):
    at = dim + left.index(bit)
    mine = bit_of(axis, bit)
    keep = lax.dynamic_index_in_dim(value, mine, at, keepdims=False)
    give = lax.dynamic_index_in_dim(value, 1 - mine, at, keepdims=False)
    total = keep.astype(F32) + partner_2(give, axis, bit).astype(F32)
    return total, [other for other in left if other != bit], give


def halved_sum(value, axis, dim, order, ties=()):
    left = list(reversed(range(bits_of(axis))))
    shape = value.shape
    value = value.reshape(shape[:dim] + (2,) * len(left) + shape[dim + 1 :])
    sent = []
    firsts = None
    for step, bit in enumerate(order):
        if step < len(ties) and ties[step] is not None:
            value = hold(value, ties[step])
        total, left, give = halve(value, axis, dim, left, bit)
        value = total.astype(BF)
        firsts = value if step == 0 else firsts
        sent.append(give)
    return total, (sent[0], firsts)


def doubled_gather(value, axis):
    shape = value.shape
    count = 0
    for bit in reversed(range(bits_of(axis))):
        other = partner_2(value, axis, bit)
        low = bit_of(axis, bit) == 0
        value = jnp.stack(
            [jnp.where(low, value, other), jnp.where(low, other, value)], axis=count
        )
        count += 1
    return value.reshape((lax.axis_size(axis),) + shape)


def exchanged_sum(value, axis):
    kind = value.dtype
    for bit in range(bits_of(axis)):
        total = value.astype(F32) + partner_2(value, axis, bit).astype(F32)
        value = total.astype(kind)
        if bit == 0:
            first = value
    return total, first


def lanes(index, width):
    return pl.ds(pl.multiple_of(index * width, width), width)


def pair_of(index, level):
    low = 2**level
    first = (index // low) * (2 * low) + index % low
    return first, first + low


def pair_matrix(w_self, w_cross, first, second):
    top = jnp.concatenate([w_self[0, first], w_cross[0, second]], axis=1)
    bottom = jnp.concatenate([w_cross[0, first], w_self[0, second]], axis=1)
    return jnp.concatenate([top, bottom], axis=0)


def side_by_side(ref, first, second, width):
    return jnp.concatenate([ref[:, lanes(first, width)], ref[:, lanes(second, width)]], axis=1)


def blocks_of(ref, first, second, width):
    per = ref.shape[2] // width
    return jnp.concatenate(
        [ref[i // per, :, lanes(lax.rem(i, per), width)] for i in (first, second)], axis=1
    )


def put_chunks(out, total):
    count, _, size = out.shape
    for chunk in range(count):
        out[chunk] = total[:, chunk * size : (chunk + 1) * size].astype(BF)


def up_kernel(levels, slots, width, pairs, hidden, w_up, *refs):
    w_self, w_cross, states = refs[:levels], refs[levels : 2 * levels], refs[2 * levels :]

    @pl.loop(0, slots, unroll=UNROLL)
    def _(j):
        both = blocks_of(hidden, pairs[j, 0], pairs[j, 1], width)
        matrix = jnp.concatenate([w_up[j, 0], w_up[j, 1]], axis=0)
        states[0][:, lanes(j, width)] = dot_nn(both, matrix).astype(BF)

    for level in range(levels):

        @pl.loop(0, slots // 2, unroll=UNROLL)
        def _(index):
            first, second = pair_of(index, level)
            both = side_by_side(states[level], first, second, width)
            result = dot_nn(both, pair_matrix(w_self[level], w_cross[level], first, second)).astype(BF)
            states[level + 1][:, lanes(first, width)] = result[:, :width]
            states[level + 1][:, lanes(second, width)] = result[:, width:]


def across_kernel(slots, width, state, partner, w_self, w_cross, out):
    @pl.loop(0, slots, unroll=UNROLL)
    def _(j):
        both = jnp.concatenate([state[:, lanes(j, width)], partner[:, lanes(j, width)]], axis=1)
        matrix = jnp.concatenate([w_self[0, j], w_cross[0, j]], axis=0)
        out[:, lanes(j, width)] = dot_nn(both, matrix).astype(BF)


def top_kernel(
    slots, width, pairs, state, partner, w_self, w_cross, w_down, cotangent, down, grad, send, total
):
    total[...] = jnp.zeros_like(total)

    @pl.loop(0, slots, unroll=UNROLL)
    def _(j):
        first, second = pairs[j, 0], pairs[j, 1]
        both = jnp.concatenate([state[:, lanes(j, width)], partner[:, lanes(j, width)]], axis=1)
        matrix = jnp.concatenate([w_self[0, j], w_cross[0, j]], axis=0)
        top = dot_nn(both, matrix).astype(BF).astype(F32)
        root = math.sqrt(2.0 / math.pi)
        square = top * top
        bend = jnp.tanh(root * (top + 0.044715 * (square * top)))
        active = (0.5 * top * (1.0 + bend)).astype(BF)
        slope = 0.5 * (1.0 + bend) + 0.5 * top * (1.0 - bend * bend) * (
            root * (1.0 + (3 * 0.044715) * square)
        )
        w_both = jnp.concatenate([w_down[j, 0], w_down[j, 1]], axis=1)
        pieces = dot_nn(active, w_both)
        total[:, lanes(first, width)] += pieces[:, :width]
        total[:, lanes(second, width)] += pieces[:, width:]
        grad_act = dot_nt(blocks_of(cotangent, first, second, width), w_both)
        grad_top = (grad_act * slope).astype(BF)
        grad[:, lanes(j, width)] = grad_top
        send[:, lanes(j, width)] = dot_nt(grad_top, w_cross[0, j]).astype(BF)

    put_chunks(down, total)


def across_grad_kernel(slots, width, state, partner, grad, after, terms):
    @pl.loop(0, slots, unroll=UNROLL)
    def _(j):
        both = jnp.concatenate([state[:, lanes(j, width)], partner[:, lanes(j, width)]], axis=1)
        result = dot_tn(both, grad[:, lanes(j, width)]).astype(BF)
        terms[0, 0, j] = result[:width]
        terms[0, 1, j] = result[width:]


def middle_kernel(slots, width, grad, incoming, w_self, w_cross_below, after, out, send):
    @pl.loop(0, slots, unroll=UNROLL)
    def _(j):
        own = dot_nt(grad[:, lanes(j, width)], w_self[0, j])
        result = (own + incoming[:, lanes(j, width)].astype(F32)).astype(BF)
        out[:, lanes(j, width)] = result
        send[:, lanes(j, width)] = dot_nt(result, w_cross_below[0, j]).astype(BF)


def down_kernel(levels, slots, width, pairs, grad, incoming, w_self_above, w_up, *refs):
    w_self, w_cross = refs[:levels], refs[levels : 2 * levels]
    grads = refs[2 * levels : 3 * levels + 1]
    spread, total = refs[3 * levels + 1 :]

    @pl.loop(0, slots, unroll=UNROLL)
    def _(j):
        own = dot_nt(grad[:, lanes(j, width)], w_self_above[0, j])
        result = own + incoming[:, lanes(j, width)].astype(F32)
        grads[levels][:, lanes(j, width)] = result.astype(BF)

    for level in reversed(range(levels)):

        @pl.loop(0, slots // 2, unroll=UNROLL)
        def _(index):
            first, second = pair_of(index, level)
            both = side_by_side(grads[level + 1], first, second, width)
            result = dot_nt(both, pair_matrix(w_self[level], w_cross[level], first, second)).astype(BF)
            grads[level][:, lanes(first, width)] = result[:, :width]
            grads[level][:, lanes(second, width)] = result[:, width:]

    total[...] = jnp.zeros_like(total)

    @pl.loop(0, slots, unroll=UNROLL)
    def _(j):
        matrix = jnp.concatenate([w_up[j, 0], w_up[j, 1]], axis=0)
        pieces = dot_nt(grads[0][:, lanes(j, width)], matrix)
        total[:, lanes(pairs[j, 0], width)] += pieces[:, :width]
        total[:, lanes(pairs[j, 1], width)] += pieces[:, width:]

    put_chunks(spread, total)


def pair_grad_kernel(group, slots, width, *refs):
    count = len(group)
    states, grads, terms = refs[:count], refs[count : 2 * count], refs[2 * count + 1]
    for at, level in enumerate(group):

        @pl.loop(0, slots // 2, unroll=UNROLL)
        def _(index):
            first, second = pair_of(index, level)
            result = dot_tn(
                side_by_side(states[at], first, second, width),
                side_by_side(grads[at], first, second, width),
            ).astype(BF)
            terms[at, 0, first] = result[:width, :width]
            terms[at, 1, second] = result[:width, width:]
            terms[at, 1, first] = result[width:, :width]
            terms[at, 0, second] = result[width:, width:]


def whole(array):
    return pl.BlockSpec(array.shape, lambda i: (0,) * array.ndim)


def level_of(array, level):
    return pl.BlockSpec((1,) + array.shape[1:], lambda i: (level, 0, 0, 0))


def rows_of(shape, tile):
    return pl.BlockSpec((tile, shape[1]), lambda i: (i, 0))


def chunk_rows_of(shape, tile):
    return pl.BlockSpec((shape[0], tile, shape[2]), lambda i: (0, i, 0))


def call(kernel, steps, operands, in_specs, out_shapes, out_specs, flops, scratch=()):
    moved = sum(x.size * x.dtype.itemsize for x in operands[:4])
    moved += sum(math.prod(x.shape) * x.dtype.itemsize for x in out_shapes)
    return pl.pallas_call(
        kernel,
        grid=(steps,),
        in_specs=in_specs,
        out_specs=out_specs,
        out_shape=out_shapes,
        scratch_shapes=scratch,
        compiler_params=pltpu.CompilerParams(vmem_limit_bytes=VMEM_BYTES),
        cost_estimate=pl.CostEstimate(flops=flops, bytes_accessed=moved, transcendentals=0),
    )(*operands)


def per_device(
    tokens, w_first, second_factor_weight, w_up, w_self, w_cross, w_down, block_pairs, cotangent
):
    seq_len, width_local = tokens.shape
    levels, slots, width, _ = w_self.shape
    model_width = width_local * lax.axis_size("tp")
    local = slots.bit_length() - 1
    hidden_width = slots * width
    total_tokens = seq_len * lax.axis_size("seq")
    token_scale = 1.0 / math.sqrt(total_tokens)
    model_width_scale = 1.0 / math.sqrt(model_width)
    positions, groups, _ = second_factor_weight.shape
    tile = seq_len // 2
    steps = 2
    smem = pl.BlockSpec(memory_space=pltpu.SMEM)
    state_shape = jax.ShapeDtypeStruct((seq_len, hidden_width), BF)
    model_shape = jax.ShapeDtypeStruct((lax.axis_size("tp"), seq_len, width_local), BF)
    seq_size = lax.axis_size("seq")

    def terms_of(count):
        return jax.ShapeDtypeStruct((count, 2, slots, width, width), BF)

    seq_bits = list(range(bits_of("seq")))
    orders = [seq_bits, seq_bits[1:2] + seq_bits[:1] + seq_bits[2:]]
    tp_bits = list(range(bits_of("tp")))

    def chunks_of(result):
        return result.reshape(result.shape[:3] + (seq_size, width // seq_size, width))

    def first_given(result, order):
        left = list(reversed(range(bits_of("seq"))))
        chunked = chunks_of(result)
        chunked = chunked.reshape(chunked.shape[:3] + (2,) * len(left) + chunked.shape[4:])
        return halve(chunked, "seq", 3, left, order[0])[2]

    def summed(result, order, ties=()):
        chunked = chunks_of(result)
        return halved_sum(chunked, "seq", 3, order, ties)[0]

    row_state = rows_of(state_shape.shape, tile)
    row_model = chunk_rows_of(model_shape.shape, tile)
    unit = 2 * seq_len * hidden_width * width

    cotangent_all = doubled_gather(cotangent, "tp")

    same = jnp.eye(positions, dtype=BF)
    mixer = (
        second_factor_weight.transpose(1, 0, 2)[:, :, :, None] * same[None, :, None, :]
    ).reshape(groups * positions, groups * positions)

    first_factor = w_first[0]
    first_out = dot_nn(first_factor, tokens).astype(BF)
    first_rows = lax.all_to_all(first_out, "seq", split_axis=0, concat_axis=0, tiled=True)
    mixed_part = dot_nn(mixer, first_rows).astype(BF)
    mixed = lax.all_to_all(mixed_part, "seq", split_axis=0, concat_axis=0, tiled=True)
    hidden_in = (tokens.astype(F32) + mixed.astype(F32)).astype(BF)
    hidden_all = doubled_gather(hidden_in, "tp")

    local_self = [w_self] * local
    local_cross = [w_cross] * local
    local_specs = [level_of(w_self, level) for level in range(local)]
    states = call(
        functools.partial(up_kernel, local, slots, width),
        steps,
        [block_pairs, hidden_all, w_up, *local_self, *local_cross],
        [smem, row_model, whole(w_up), *local_specs, *local_specs],
        [state_shape] * (local + 1),
        [row_state] * (local + 1),
        (local + 1) * 2 * unit,
    )
    states = list(states)
    partners = [None] * levels
    for level in range(local, levels - 1):
        partners[level] = partner_2(states[level], "tp", level - local)
        (state,) = call(
            functools.partial(across_kernel, slots, width),
            steps,
            [states[level], partners[level], w_self, w_cross],
            [row_state, row_state, level_of(w_self, level), level_of(w_cross, level)],
            [state_shape],
            [row_state],
            2 * unit,
        )
        states.append(state)
    last = levels - 1
    partners[last] = partner_2(states[last], "tp", last - local)
    down_part, grad, send = call(
        functools.partial(top_kernel, slots, width),
        steps,
        [block_pairs, states[last], partners[last], w_self, w_cross, w_down, cotangent_all],
        [
            smem,
            row_state,
            row_state,
            level_of(w_self, last),
            level_of(w_cross, last),
            whole(w_down),
            row_model,
        ],
        [model_shape, state_shape, state_shape],
        [row_model, row_state, row_state],
        7 * unit,
        [pltpu.VMEM((tile, model_width), F32)],
    )
    terms = [None] * levels

    anywhere = pl.BlockSpec(memory_space=pl.ANY)

    def across_terms(level, gradient, after):
        (result,) = call(
            functools.partial(across_grad_kernel, slots, width),
            1,
            [states[level], partners[level], gradient, after],
            [whole(states[level]), whole(states[level]), whole(gradient), anywhere],
            [terms_of(1)],
            [whole(terms_of(1))],
            2 * unit,
        )
        return result

    early = []
    for level in range(last, local, -1):
        incoming = partner_2(send, "tp", level - local)
        result = across_terms(level, grad, send)
        early.append((level, result))
        given = first_given(result, orders[level % 2])
        grad, send = call(
            functools.partial(middle_kernel, slots, width),
            steps,
            [grad, incoming, w_self, w_cross, given],
            [
                row_state,
                row_state,
                level_of(w_self, level),
                level_of(w_cross, level - 1),
                anywhere,
            ],
            [state_shape, state_shape],
            [row_state, row_state],
            2 * unit,
        )
    incoming = partner_2(send, "tp", 0)
    grad_above = grad
    *grads, spread = call(
        functools.partial(down_kernel, local, slots, width),
        steps,
        [block_pairs, grad, incoming, w_self, w_up, *local_self, *local_cross],
        [
            smem,
            row_state,
            row_state,
            level_of(w_self, local),
            whole(w_up),
            *local_specs,
            *local_specs,
        ],
        [state_shape] * (local + 1) + [model_shape],
        [row_state] * (local + 1) + [row_model],
        (2 * local + 3) * unit,
        [pltpu.VMEM((tile, model_width), F32)],
    )
    spread_part, (spread_sent, spread_first) = halved_sum(spread, "tp", 0, tp_bits)
    grad_hidden = (cotangent.astype(F32) + spread_part).astype(BF)
    down_sum, _ = halved_sum(down_part, "tp", 0, tp_bits)
    layer_out = (hidden_in.astype(F32) + down_sum).astype(BF)

    grad_rows = lax.all_to_all(grad_hidden, "seq", split_axis=0, concat_axis=0, tiled=True)
    moved_back = dot_tn(mixer, grad_rows).astype(BF)
    returned = lax.all_to_all(moved_back, "seq", split_axis=0, concat_axis=0, tiled=True)
    first_part = dot_nt(returned, tokens).astype(BF)
    first_sum, first_hop = exchanged_sum(first_part, "tp")
    ties = [None, grad_rows, first_hop]
    for level, result in early:
        terms[level] = summed(result, orders[level % 2])[0]
    result = across_terms(local, grad_above, spread_sent)
    terms[local] = summed(result, orders[local % 2], ties)[0]
    for top in range(local, 0, -2):
        group = list(range(max(top - 2, 0), top))
        (result,) = call(
            functools.partial(pair_grad_kernel, group, slots, width),
            1,
            [states[level] for level in group]
            + [grads[level + 1] for level in group]
            + [spread_first],
            [whole(states[0])] * (2 * len(group)) + [anywhere],
            [terms_of(len(group))],
            [whole(terms_of(len(group)))],
            2 * len(group) * unit,
        )
        sums = summed(result, orders[(local - top) // 2 % 2], ties)
        for at, level in enumerate(group):
            terms[level] = sums[at]

    cross_rows = dot_nt(grad_rows, first_rows).reshape(groups, positions, groups, positions)
    second_part = jnp.sum(cross_rows * same.astype(F32)[None, :, None, :], axis=3).transpose(1, 0, 2)
    second_sum, _ = exchanged_sum(second_part, "tp")
    grad_mix = dot_tn(first_factor, returned)
    grad_tokens = (grad_hidden.astype(F32) + grad_mix).astype(BF)
    level_terms = jnp.stack(terms, axis=1) * token_scale
    return (
        layer_out,
        grad_tokens,
        (first_sum * model_width_scale)[None],
        second_sum * model_width_scale,
        level_terms[0],
        level_terms[1],
    )


def solution(mesh):
    in_specs = (
        P("seq", "tp"),
        P("seq", None, None),
        P("seq", None, None),
        P("tp", None, None, None),
        P(None, "tp", None, None),
        P(None, "tp", None, None),
        P("tp", None, None, None),
        P("tp", None),
        P("seq", "tp"),
    )
    out_specs = (
        P("seq", "tp"),
        P("seq", "tp"),
        P("seq", None, None),
        P("seq", None, None),
        P(None, "tp", "seq", None),
        P(None, "tp", "seq", None),
    )
    return jax.shard_map(
        per_device, mesh=mesh, in_specs=in_specs, out_specs=out_specs, check_vma=False
    )
```
